32 devices in a mesh: grp: 2 (over y), blk: 16 (over z, x, core).
Axes of the slice: x: 2, y: 2, z: 4, core: 2. Of those that a mesh axis runs over, the one named last changes fastest.
Arguments:
- activations: bfloat16 [2, 4096, 8192], P(None, ('grp', 'blk')), parts along dimension 1, may hold values from -6 to 6
- backprops: bfloat16 [2, 4096, 8192], P(None, ('grp', 'blk')), parts along dimension 1, may hold values from -6 to 6
- out_factors: bfloat16 [2, 384, 8192], P(None, 'blk'), may hold values from -1 to 1
- in_factors: bfloat16 [2, 384, 8192], P(None, 'blk'), may hold values from -1 to 1
- lengths: int32 [2], P('grp'), parts along dimension 0, may hold values from 512 to 2048, as said below
Outputs:
- layer_scores: float32 [2, 2, 12], P(None, 'grp'), parts along dimension 1
The draws below stay inside these ranges and needn't reach their ends.
There are 2 independent parts, one for each index of `grp`. The reference program is written for one: setup_inputs(seed, part) draws one part's arguments, and reference() takes and returns one part's arrays. A program takes and returns all parts, laid end to end along the dimension named above; an argument that names none is the same for every part. Nothing has to cross between parts.
Inputs may be any that keep to these rules, and one draw needn't show every extreme that they name: `lengths`: some sequence has all 2048 tokens used in every draw.
All inputs are finite; a program needn't handle non-finite values.
Results may differ from the reference program's by a relative error of at most 0.0004.
Values may be sent and summed in bfloat16 or wider, within the bound.
No kernel may reach another device: no remote copies, remote signals or barrier semaphores. Data moves between devices by JAX's collectives and lax.ppermute only.
A program may use at most 128 MiB of HBM per device.

```python
import jax
import jax.numpy as jnp

DIN = 8192
DOUT = 8192
RANK = 32
QUERIES = 12
LAYERS = 2
LEN = 2048
TOKENS = 2048
SEQS = 1


def shared_tokens(key):
    return jnp.clip(jax.random.normal(key, (LAYERS, TOKENS, DIN), jnp.float32), -6.0, 6.0)


def shared_columns(key):
    return jax.random.normal(key, (LAYERS, QUERIES * RANK, DOUT), jnp.float32)


def draw_activations(key, part):
    common = shared_tokens(key)
    return common.astype(jnp.bfloat16)


def draw_backprops(key, part):
    common = shared_tokens(key)
    key = jax.random.fold_in(key, 11)
    noise = jax.random.normal(key, (LAYERS, TOKENS, DOUT), jnp.float32)
    return jnp.clip(0.6 * common + 0.8 * noise, -6.0, 6.0).astype(jnp.bfloat16)


def draw_out_factors(key, part):
    common = shared_columns(key)
    return jnp.clip(common * DOUT ** (-0.5), -1.0, 1.0).astype(jnp.bfloat16)


def draw_in_factors(key, part):
    common = shared_columns(key)
    key = jax.random.fold_in(key, 13)
    sign_key, noise_key = jax.random.split(key)
    column_scale = jax.random.normal(sign_key, (LAYERS, QUERIES * RANK, 1), jnp.float32)
    noise = jax.random.normal(noise_key, (LAYERS, QUERIES * RANK, DIN), jnp.float32)
    factor = 1.0 / (0.36 * LEN * RANK ** 0.5)
    values = factor * (0.6 * column_scale * common + 0.8 * noise) * DIN ** (-0.5)
    return jnp.clip(values, -1.0, 1.0).astype(jnp.bfloat16)


def draw_lengths(key, part):
    key = jax.random.fold_in(key, 7)
    first_key, second_key = jax.random.split(key)
    values = jax.random.randint(first_key, (SEQS,), LEN // 4, LEN + 1)
    chosen = jax.random.randint(second_key, (), 0, SEQS)
    return jnp.where(jnp.arange(SEQS) == chosen, LEN, values).astype(jnp.int32)


def setup_inputs(seed: int = 0, part: int = 0) -> dict:
    key_of = jax.random.split(jax.random.key(seed), 6)
    own_keys = jax.random.split(jax.random.fold_in(key_of[5], part), 6)
    return {
        "activations": draw_activations(jax.random.fold_in(jax.random.fold_in(key_of[5], part), 71), part),
        "backprops": draw_backprops(jax.random.fold_in(jax.random.fold_in(key_of[5], part), 71), part),
        "out_factors": draw_out_factors(jax.random.fold_in(key_of[5], 71), part),
        "in_factors": draw_in_factors(jax.random.fold_in(key_of[5], 71), part),
        "lengths": draw_lengths(jax.random.fold_in(jax.random.fold_in(key_of[5], part), 71), part),
    }


def reference(activations, backprops, out_factors, in_factors, lengths):
    position = jnp.arange(TOKENS, dtype=jnp.int32)
    sequence_of = (position // LEN).astype(jnp.int32)
    in_use = ((position % LEN) < lengths[sequence_of]).astype(jnp.float32)
    results = []
    for layer in range(LAYERS):
        proj_out = jnp.dot(backprops[layer], out_factors[layer].T, preferred_element_type=jnp.float32)
        proj_in = jnp.dot(activations[layer], in_factors[layer].T, preferred_element_type=jnp.float32)
        product = proj_out * proj_in * in_use[:, None]
        results.append(product.reshape(SEQS, LEN, QUERIES, RANK).sum(axis=(1, 3)))
    return jnp.stack(results)
```

```python
import jax
import jax.numpy as jnp
from jax import lax
from jax.experimental import pallas as pl
from jax.experimental.pallas import tpu as pltpu
from jax.sharding import PartitionSpec as P

RANK = 32
LEN = 2048


def chip_ring(chips):
    return list(range(0, chips, 2)) + list(range(chips - 1, 0, -2))


def project(factors, tokens):
    return lax.dot_general(
        factors, tokens, (((1,), (1,)), ((), ())), preferred_element_type=jnp.float32
    )


def move(sources, targets, after=()):
    count = len(sources)
    moves, shapes = [], []
    for t, ranges in enumerate(targets):
        offset = 0
        for s, layer, start, stop in ranges:
            moves.append((t, s, layer, start, stop, offset))
            offset += stop - start
        lead = sources[s].shape[:2] if layer is None else sources[s].shape[1:2]
        shapes.append(jax.ShapeDtypeStruct((*lead, offset), sources[s].dtype))

    def kernel(*refs):
        ins, outs, sems = refs[:count], refs[count + len(after) : -1], refs[-1]
        me = lax.axis_index("grp")
        copies = []
        for k, (t, s, layer, start, stop, offset) in enumerate(moves):
            columns, place = pl.ds(start, stop - start), pl.ds(offset, stop - start)
            if layer is None:
                source, target = ins[s].at[:, :, columns], outs[t].at[:, :, place]
            else:
                row = me if layer == "mine" else 1 - me
                source, target = ins[s].at[row, :, columns], outs[t].at[:, place]
            copies.append(pltpu.make_async_copy(source, target, sems.at[k]))
            copies[-1].start()
        for copy in copies:
            copy.wait()

    anywhere = pl.BlockSpec(memory_space=pl.ANY)
    return pl.pallas_call(
        kernel,
        out_shape=shapes,
        in_specs=[anywhere] * (count + len(after)),
        out_specs=[pl.BlockSpec(memory_space=pltpu.VMEM)] * len(shapes),
        scratch_shapes=[pltpu.SemaphoreType.DMA((len(moves),))],
        compiler_params=pltpu.CompilerParams(vmem_limit_bytes=16 * 2**20),
    )(*sources, *after)


def cuts(total, parts):
    edges = [0]
    for k in range(1, parts):
        edges.append(total * 2 * k // (2 * parts - 1) // 128 * 128)
    return edges + [total]


def solution(mesh):
    blk = mesh.shape["blk"]
    chips = blk // 2
    full = (chips - 1) // 2
    order = chip_ring(chips)
    forward, backward = [], []
    for core in range(2):
        for k in range(chips):
            a = order[k] * 2 + core
            b = order[(k + 1) % chips] * 2 + core
            forward.append((a, b))
            backward.append((b, a))
    place = [0] * chips
    for k, chip in enumerate(order):
        place[chip] = k

    def swap_core(x):
        return lax.ppermute(x, "blk", [(i, i ^ 1) for i in range(blk)])

    def swap_grp(x):
        return lax.ppermute(x, "grp", [(0, 1), (1, 0)])

    def gather(piece, halves, chunks):
        ahead = back = piece
        got, tokens, swapped, state = [piece], [], [], ()
        for step in range(full + 1):
            send = (ahead, back) if step < full else halves(ahead, back)
            chunk = chunks(step)
            if chunk is not None:
                send = lax.optimization_barrier((*send, chunk, *state))
                chunk = send[2]
            ahead = lax.ppermute(send[0], "blk", forward)
            back = lax.ppermute(send[1], "blk", backward)
            state = (ahead, back)
            if chunk is not None:
                if tokens:
                    swapped.append(swap_core(tokens[-1]))
                tokens.append(swap_grp(chunk))
                state += (tokens[-1], *swapped[-1:])
            if step < full:
                got += [ahead, back]
            yield state
        swapped.append(swap_core(tokens[-1]))
        yield got, (ahead, back), tokens, swapped

    def shards(activations, backprops, out_factors, in_factors, lengths):
        tokens_here = activations.shape[1]
        width = backprops.shape[2]
        depth = activations.shape[2]
        cut = depth * 9 // 16
        packed = width + cut
        columns = out_factors.shape[1]
        seq_count = lengths.shape[0]
        me = lax.axis_index("grp")
        device = lax.axis_index("blk")

        def layer_of(x, layer):
            return lax.dynamic_index_in_dim(x, layer, 0, keepdims=False)

        home_rate, rate = 2 * (depth - cut), packed
        near = packed * rate // (rate + home_rate) // 128 * 128
        parts = min(full + 1, 4)
        near_edges = cuts(near, parts)
        far_edges = [near + e for e in cuts(packed - near, parts)]

        def packing(out_source, in_source, layer, start, stop):
            ranges = []
            if start < width:
                ranges.append((out_source, layer, start, min(stop, width)))
            if stop > width:
                ranges.append((in_source, layer, max(start - width, 0), stop - width))
            return ranges

        def away_part(edges, k):
            return packing(1, 0, "other", edges[k], edges[k + 1])

        tokens = (activations, backprops)
        home_piece, far_first = move(
            (activations, backprops, in_factors),
            [[(2, None, cut, depth)], away_part(far_edges, 0)],
        )
        piece, near_first, far_second = move(
            (*tokens, in_factors, out_factors),
            [
                packing(3, 2, "mine", 0, packed),
                away_part(near_edges, 0),
                away_part(far_edges, 1),
            ],
            after=(home_piece,),
        )
        later = {}
        home_ring = gather(
            home_piece,
            lambda a, b: (a[:1], b[1:]),
            lambda k: [far_first, far_second, *later.get("far", ())][k] if k < parts else None,
        )
        state = next(home_ring)
        rest = [away_part(near_edges, 1)]
        for k in range(2, parts):
            rest += [away_part(far_edges, k), away_part(near_edges, k)]
        rest += [packing(1, 0, "mine", 0, packed), [(0, None, cut, depth)]]
        moved = move(tokens, rest, after=state[:1])
        later["near"], later["far"] = moved[0:-2:2], moved[1:-2:2]
        mine, home_tokens = moved[-2:]
        for state in home_ring:
            pass
        home_got, home_last, far_away, far_sib = state
        home_got.append(jnp.concatenate(home_last, axis=0))
        middle = packed // 2
        for state in gather(
            piece,
            lambda a, b: (a[:, :middle], b[:, middle:]),
            lambda k: [near_first, *later["near"]][k] if k < parts else None,
        ):
            pass
        got, last, near_away, near_sib = state
        got.append(jnp.concatenate(last, axis=1))

        mine_sib = swap_core(mine)
        home_sib = swap_core(home_tokens)
        away = jnp.concatenate(near_away + far_away, axis=1)
        away_sib = jnp.concatenate(near_sib + far_sib, axis=1)
        other_lengths = swap_grp(lengths)

        home_factors = jnp.concatenate(home_got, axis=1)

        def home(tokens):
            return jnp.einsum(
                "lkd,ltd->lkt", home_factors, tokens, preferred_element_type=jnp.float32
            )

        home = jnp.concatenate([home(home_tokens), home(home_sib)], axis=2)
        home_mine = layer_of(home, me)
        home_away = swap_grp(layer_of(home, 1 - me))

        factors = jnp.concatenate(got, axis=0)
        first = (device // 2) * 2 * tokens_here
        sequence = first // LEN
        select = jnp.arange(seq_count, dtype=jnp.int32) == sequence
        odd = device % 2
        start = first % LEN

        def score(own, sib, beyond, limits):
            limit = jnp.sum(jnp.where(select, limits, 0))
            total = 0.0
            for k, tokens in enumerate((own, sib)):
                proj_out = project(factors[:, :width], tokens[:, :width])
                proj_in = project(factors[:, width:], tokens[:, width:])
                proj_in += beyond[:, k * tokens_here : (k + 1) * tokens_here]
                position = (
                    start
                    + (odd ^ k) * tokens_here
                    + jnp.arange(tokens_here, dtype=jnp.int32)
                )
                in_use = (position < limit).astype(jnp.float32)
                total += jnp.sum(proj_out * proj_in * in_use[None, :], axis=1)
            return total

        per_column = jnp.stack(
            [
                score(mine, mine_sib, home_mine, lengths),
                score(away, away_sib, home_away, other_lengths),
            ]
        )

        at = jnp.asarray(place, jnp.int32)[device // 2]
        steps = [0]
        for k in range(1, full + 1):
            steps += [-k, k]
        steps.append(chips // 2)
        shard_chip = jnp.asarray(order, jnp.int32)[
            (at + jnp.asarray(steps, jnp.int32)) % chips
        ]
        first_column = (shard_chip * 2 + odd) * columns
        column = first_column[:, None] + jnp.arange(columns, dtype=jnp.int32)[None, :]
        query = column.reshape(-1) // RANK
        queries = columns * blk // RANK
        hit = (query[:, None] == jnp.arange(queries)[None, :]).astype(jnp.float32)
        per_query = jnp.sum(per_column[:, :, None] * hit[None], axis=1)

        other = swap_grp(per_query[1])
        rows = jnp.arange(2)[:, None] == me
        value = jnp.where(rows, per_query[0][None], other[None])
        value = value[:, None, :] * select.astype(jnp.float32)[None, :, None]
        if blk & (blk - 1):
            return lax.psum(value, "blk")
        bit = 1
        while bit < blk:
            value = value + lax.ppermute(value, "blk", [(i, i ^ bit) for i in range(blk)])
            bit *= 2
        return value

    placed = (
        P(None, ("grp", "blk"), None),
        P(None, ("grp", "blk"), None),
        P(None, "blk", None),
        P(None, "blk", None),
        P("grp"),
    )
    return jax.shard_map(
        shards, mesh=mesh, in_specs=placed, out_specs=P(None, "grp", None), check_vma=False
    )
```

```python
import math

import jax
import jax.numpy as jnp
from jax import lax
from jax.experimental import pallas as pl
from jax.experimental.pallas import tpu as pltpu
from jax.sharding import PartitionSpec as P

RANK = 32
LEN = 2048
MIB = 2**20
SPAN = 512
LOAD = 2048
OUTER = 52
ANYWHERE = pl.BlockSpec(memory_space=pl.ANY)
CHIP = pl.BlockSpec(memory_space=pltpu.VMEM)


def chip_ring(chips):
    return list(range(0, chips, 2)) + list(range(chips - 1, 0, -2))


def contract(factors, tokens):
    return lax.dot_general(
        factors, tokens, (((1,), (1,)), ((), ())), preferred_element_type=jnp.float32
    )


def rows_of(pieces):
    return jnp.concatenate(pieces, axis=0) if len(pieces) > 1 else pieces[0]


def move(sources, targets, after=()):
    count = len(sources)
    moves, shapes = [], []
    for t, ranges in enumerate(targets):
        offset = 0
        for s, layer, start, stop in ranges:
            moves.append((t, s, layer, start, stop, offset))
            offset += stop - start
        lead = sources[s].shape[:2] if layer is None else sources[s].shape[1:2]
        shapes.append(jax.ShapeDtypeStruct((*lead, offset), sources[s].dtype))

    def kernel(*refs):
        ins, outs, sems = refs[:count], refs[count + len(after) : -1], refs[-1]
        me = lax.axis_index("grp")
        copies = []
        for k, (t, s, layer, start, stop, offset) in enumerate(moves):
            columns, place = pl.ds(start, stop - start), pl.ds(offset, stop - start)
            if layer is None:
                source, target = ins[s].at[:, :, columns], outs[t].at[:, :, place]
            else:
                row = {"mine": me, "other": 1 - me}.get(layer, layer)
                source, target = ins[s].at[row, :, columns], outs[t].at[:, place]
            copies.append(pltpu.make_async_copy(source, target, sems.at[k]))
            copies[-1].start()
        for copy in copies:
            copy.wait()

    return pl.pallas_call(
        kernel,
        out_shape=shapes,
        in_specs=[ANYWHERE] * (count + len(after)),
        out_specs=[CHIP] * len(shapes),
        scratch_shapes=[pltpu.SemaphoreType.DMA((len(moves),))],
        compiler_params=pltpu.CompilerParams(vmem_limit_bytes=62 * MIB),
        cost_estimate=pl.CostEstimate(
            flops=0,
            transcendentals=0,
            bytes_accessed=4 * sum(math.prod(x.shape) * 2 for x in shapes),
        ),
    )(*sources, *after)


def cost(flops):
    return pl.CostEstimate(flops=flops, transcendentals=0, bytes_accessed=flops // 64)


class Loads:

    def __init__(self):
        self.arrays, self.keys, self.targets = [], [], []

    def add(self, array, lead, first, width, target=None):
        for k, known in enumerate(self.arrays):
            if known is array:
                break
        else:
            k = len(self.arrays)
            self.arrays.append(array)
        self.keys.append((k, lead, first, width))
        self.targets.append(target)
        return len(self.keys) - 1

    def scratch(self):
        buffers = [
            pltpu.VMEM((self.arrays[k].shape[-2], width), self.arrays[k].dtype)
            for (k, _, _, width), target in zip(self.keys, self.targets)
            if target is None
        ]
        return [*buffers, pltpu.SemaphoreType.DMA((len(self.keys),))]

    def start(self, ins, outs, buffers):
        free = iter(buffers[:-1])
        self.copies, self.refs = [], []
        for i, ((k, lead, first, width), target) in enumerate(zip(self.keys, self.targets)):
            columns = pl.ds(first, width)
            row = lax.axis_index("grp") if lead == "mine" else lead
            source = ins[k].at[:, columns] if lead is None else ins[k].at[row, :, columns]
            if target is None:
                ref = next(free)
            else:
                out, down, across = target
                rows = self.arrays[k].shape[-2]
                ref = outs[out].at[pl.ds(down, rows), pl.ds(across, width)]
            self.refs.append(ref)
            self.copies.append(pltpu.make_async_copy(source, ref, buffers[-1].at[i]))
            self.copies[-1].start()

    def wait(self, wanted=None):
        for i in sorted(set(range(len(self.keys)) if wanted is None else wanted)):
            if self.copies[i] is not None:
                self.copies[i].wait()
                self.copies[i] = None


def products(total, factors, tokens, width):
    for a in range(0, width, SPAN):
        span = min(SPAN, width - a)
        left = rows_of([ref[:, first + a : first + a + span] for ref, first in factors])
        right = rows_of([ref[:, first + a : first + a + span] for ref, first in tokens])
        product = contract(left, right)
        total = product if total is None else total + product
    return total


def solution(mesh):
    blk = mesh.shape["blk"]
    chips = blk // 2
    full = (chips - 1) // 2
    order = chip_ring(chips)
    forward, backward = [], []
    for core in range(2):
        for k in range(chips):
            a = order[k] * 2 + core
            b = order[(k + 1) % chips] * 2 + core
            forward.append((a, b))
            backward.append((b, a))
    place = [0] * chips
    for k, chip in enumerate(order):
        place[chip] = k

    def swap_core(x):
        return lax.ppermute(x, "blk", [(i, i ^ 1) for i in range(blk)])

    def swap_grp(x):
        return lax.ppermute(x, "grp", [(0, 1), (1, 0)])

    def ahead_of(x):
        return lax.ppermute(x, "blk", forward)

    def back_of(x):
        return lax.ppermute(x, "blk", backward)

    def after(values, *others):
        return lax.optimization_barrier((*values, *others))[: len(values)]

    def shards(activations, backprops, out_factors, in_factors, lengths):
        tokens_here = activations.shape[1]
        width = backprops.shape[2]
        depth = activations.shape[2]
        cut = depth * 7 // 16
        packed = width + cut
        beyond = depth - cut
        columns = out_factors.shape[1]
        seq_count = lengths.shape[0]
        me = lax.axis_index("grp")
        device = lax.axis_index("blk")

        def packing(out_source, in_source, layer, start, stop):
            ranges = []
            if start < width:
                ranges.append((out_source, layer, start, min(stop, width)))
            if stop > width:
                ranges.append((in_source, layer, max(start - width, 0), stop - width))
            return ranges

        share = -(-packed // 3 // 128) * 128
        edges = [0, share, 2 * share, packed]

        def away_part(k):
            return packing(1, 0, "other", edges[k], edges[k + 1])

        acts_sib, backs_sib = swap_core(activations), swap_core(backprops)

        sources = (activations, backprops)
        piece, *chunks = move(
            (*sources, out_factors, in_factors),
            [
                packing(2, 3, "mine", 0, packed) + [(3, k, cut, depth) for k in range(2)],
                away_part(0),
            ],
        )
        chunks += move(sources, [away_part(1), away_part(2)], after=(piece,))

        got = [piece]
        ahead = back = piece
        away, away_sib = [], []
        for step in range(full):
            given = [ahead, back]
            if step < 3:
                given.append(chunks[step])
            if step == 1:
                given = after(given, away[0], *chunks[1:], backs_sib)
            if step == 2:
                given = after(given, away[1], acts_sib)
                away_sib = [swap_core(x) for x in away]
            ahead, back = ahead_of(given[0]), back_of(given[1])
            if step < 3:
                away.append(swap_grp(given[2]))
            got += [ahead, back]
        ahead, back = after((ahead, back), away[2], *away_sib)
        away_sib.append(swap_core(away[2]))
        last_home = (
            ahead_of(ahead[:, packed : packed + beyond]),
            back_of(back[:, packed + beyond :]),
        )
        middle = packed // 2
        rest = after((ahead[:, :middle], back[:, middle:packed]), *last_home)
        last = ahead_of(rest[0]), back_of(rest[1])
        if chips > 8:
            got = [jnp.concatenate(got, axis=0)]

        shard_rows = chips * columns
        chip_tokens = 2 * tokens_here

        home_loads = Loads()
        home_shards = [home_loads.add(g, None, packed, 2 * beyond) for g in got]
        home_sides = []
        for k in range(2):
            home_sides.append(
                (
                    home_loads.add(last_home[k], None, 0, beyond),
                    [home_loads.add(x, k, cut, beyond) for x in (activations, acts_sib)],
                )
            )
        count_home = len(home_loads.arrays)

        def home_kernel(*refs):
            lengths_ref, mine_ref, other_ref, *scratch = refs[count_home:]
            home_loads.start(refs[:count_home], (), scratch)
            at = home_loads.refs
            me = lax.axis_index("grp")
            first = lax.axis_index("blk") // 2 * chip_tokens
            limit = lengths_ref[first // LEN].astype(jnp.float32)
            for ref in (mine_ref, other_ref):
                ref[shard_rows:, :] = jnp.full((8, chip_tokens), limit)
            for k, (tail, tokens) in enumerate(home_sides):
                home_loads.wait([*home_shards, tail, *tokens])
                factors = [(at[i], k * beyond) for i in home_shards] + [(at[tail], 0)]
                value = products(None, factors, [(at[i], 0) for i in tokens], beyond)

                @pl.when(me == k)
                def _():
                    mine_ref[:shard_rows, :] = value

                @pl.when(me != k)
                def _():
                    other_ref[:shard_rows, :] = value

        extra = jax.ShapeDtypeStruct((shard_rows + 8, chip_tokens), jnp.float32)
        home_mine, home_away = pl.pallas_call(
            home_kernel,
            out_shape=[extra] * 2,
            in_specs=[ANYWHERE] * count_home + [pl.BlockSpec(memory_space=pltpu.SMEM)],
            out_specs=[CHIP] * 2,
            scratch_shapes=home_loads.scratch(),
            compiler_params=pltpu.CompilerParams(vmem_limit_bytes=62 * MIB),
            cost_estimate=cost(2 * shard_rows * chip_tokens * 2 * beyond),
        )(*home_loads.arrays, lengths)
        home_away = swap_grp(home_away)

        points = sorted({*range(0, packed, LOAD), width, middle, *edges})
        loads = Loads()
        plan, shard_loads = [], {}
        for a, b in zip(points[:-1], points[1:]):
            k = max(i for i in range(3) if edges[i] <= a)
            if a >= width:
                break
            base = 0 if a < width // 2 else width // 2
            if base not in shard_loads:
                shard_loads[base] = [loads.add(g, None, base, width // 2) for g in got]
            if a < middle:
                tail = loads.add(last[0], None, a, b - a)
            else:
                tail = loads.add(last[1], None, a - middle, b - a)
            tokens = [loads.add(x, "mine", a, b - a) for x in (backprops, backs_sib)]
            tokens += [loads.add(x[k], None, a - edges[k], b - a) for x in (away, away_sib)]
            plan.append((base, a, b, tail, tokens))
        for i, x in enumerate((activations, acts_sib)):
            loads.add(x, "mine", 0, cut, (1, i * tokens_here, 0))
        for k in range(3):
            a, b = max(edges[k], width), edges[k + 1]
            if a < b:
                for i, x in enumerate((away, away_sib)):
                    loads.add(
                        x[k], None, a - edges[k], b - a, (1, (2 + i) * tokens_here, a - width)
                    )
        for i, g in enumerate(got):
            loads.add(g, None, width, cut, (2 + i, 0, 0))
        count = len(loads.arrays)
        outs = 2 + len(got)

        def out_kernel(*refs):
            out_refs = refs[count : count + outs]
            loads.start(refs[:count], out_refs, refs[count + outs :])
            at, total = loads.refs, None
            for base, a, b, tail, tokens in plan:
                loads.wait([*shard_loads[base], tail, *tokens])
                factors = [(at[i], a - base) for i in shard_loads[base]] + [(at[tail], 0)]
                total = products(total, factors, [(at[i], 0) for i in tokens], b - a)
            out_refs[0][...] = total
            loads.wait()

        proj_out, in_tokens, *in_shards = pl.pallas_call(
            out_kernel,
            out_shape=[
                jax.ShapeDtypeStruct((shard_rows, 2 * chip_tokens), jnp.float32),
                jax.ShapeDtypeStruct((2 * chip_tokens, cut), activations.dtype),
                *(jax.ShapeDtypeStruct((g.shape[0], cut), g.dtype) for g in got),
            ],
            in_specs=[ANYWHERE] * count,
            out_specs=[CHIP] * outs,
            scratch_shapes=loads.scratch(),
            compiler_params=pltpu.CompilerParams(vmem_limit_bytes=OUTER * MIB),
            cost_estimate=cost(2 * shard_rows * 2 * chip_tokens * width),
        )(*loads.arrays)

        odd = device % 2
        at = jnp.asarray(place, jnp.int32)[device // 2]
        steps = [0]
        for k in range(1, full + 1):
            steps += [-k, k]
        steps.append(chips // 2)
        shard_chip = jnp.asarray(order, jnp.int32)[
            (at + jnp.asarray(steps, jnp.int32)) % chips
        ]
        first_column = (shard_chip * 2 + odd) * columns
        column = first_column[:, None] + jnp.arange(columns, dtype=jnp.int32)[None, :]
        query = column.reshape(-1) // RANK
        queries = columns * blk // RANK
        hit = (query[:, None] == jnp.arange(128)[None, :]).astype(jnp.float32)

        shards_in = len(in_shards)
        tail_in = last[1] if middle <= width else None
        assert tail_in is not None

        def score_kernel(*refs):
            token_ref, tail_ref = refs[shards_in : shards_in + 2]
            out_ref, mine_ref, other_ref, hit_ref, *scores = refs[shards_in + 2 :]
            factors = [(ref, 0) for ref in refs[:shards_in]] + [(tail_ref, width - middle)]
            proj_in = products(None, factors, [(token_ref, 0)], cut)
            first = lax.axis_index("blk") // 2 * chip_tokens
            flip = lax.axis_index("blk") % 2
            lane = lax.broadcasted_iota(jnp.int32, (1, chip_tokens), 1)
            swapped = jnp.where(lane < tokens_here, lane + tokens_here, lane - tokens_here)
            position = (first % LEN + jnp.where(flip == 1, swapped, lane)).astype(jnp.float32)

            for k, extra_ref in enumerate((mine_ref, other_ref)):
                span = slice(k * chip_tokens, (k + 1) * chip_tokens)
                in_use = position < extra_ref[shard_rows : shard_rows + 1, :]
                product = out_ref[:, span] * (proj_in[:, span] + extra_ref[:shard_rows, :])
                product = jnp.where(in_use, product, 0.0)
                per_column = jnp.sum(product, axis=1, keepdims=True)
                scores[k][...] = jnp.sum(per_column * hit_ref[...], axis=0, keepdims=True)

        own, other = pl.pallas_call(
            score_kernel,
            out_shape=[jax.ShapeDtypeStruct((1, 128), jnp.float32)] * 2,
            in_specs=[CHIP] * (shards_in + 6),
            out_specs=[CHIP] * 2,
            compiler_params=pltpu.CompilerParams(vmem_limit_bytes=OUTER * MIB),
            cost_estimate=cost(2 * shard_rows * 2 * chip_tokens * cut),
        )(*in_shards, in_tokens, last[1], proj_out, home_mine, home_away, hit)

        other = swap_grp(other)
        sequence = device // 2 * chip_tokens // LEN
        select = jnp.arange(seq_count, dtype=jnp.int32) == sequence
        rows = jnp.arange(2)[:, None] == me
        value = jnp.where(rows, own, other)
        value = value[:, None, :] * select.astype(jnp.float32)[None, :, None]
        if blk & (blk - 1):
            return lax.psum(value, "blk")[:, :, :queries]
        bit = 1
        while bit < blk:
            value = value + lax.ppermute(value, "blk", [(i, i ^ bit) for i in range(blk)])
            bit *= 2
        return value[:, :, :queries]

    placed = (
        P(None, ("grp", "blk"), None),
        P(None, ("grp", "blk"), None),
        P(None, "blk", None),
        P(None, "blk", None),
        P("grp"),
    )
    return jax.shard_map(
        shards, mesh=mesh, in_specs=placed, out_specs=P(None, "grp", None), check_vma=False
    )
```

```python
import math

import jax
import jax.numpy as jnp
from jax import lax
from jax.experimental import pallas as pl
from jax.experimental.pallas import tpu as pltpu
from jax.sharding import PartitionSpec as P

RANK = 32
LEN = 2048
MIB = 2**20
SPAN = 512
RESERVE = 8
OUTER = 50
ANYWHERE = pl.BlockSpec(memory_space=pl.ANY)
CHIP = pl.BlockSpec(memory_space=pltpu.VMEM)


def chip_ring(chips):
    return list(range(0, chips, 2)) + list(range(chips - 1, 0, -2))


def contract(left, right):
    return lax.dot_general(
        left, right, (((1,), (1,)), ((), ())), preferred_element_type=jnp.float32
    )


def rows_of(pieces):
    return jnp.concatenate(pieces, axis=0) if len(pieces) > 1 else pieces[0]


def move(sources, targets, after=()):
    count = len(sources)
    moves, shapes = [], []
    for t, ranges in enumerate(targets):
        offset = 0
        for s, layer, start, stop in ranges:
            moves.append((t, s, layer, start, stop, offset))
            offset += stop - start
        lead = sources[s].shape[:2] if layer is None else sources[s].shape[1:2]
        shapes.append(jax.ShapeDtypeStruct((*lead, offset), sources[s].dtype))

    def kernel(*refs):
        ins, outs, sems = refs[:count], refs[count + len(after) : -1], refs[-1]
        me = lax.axis_index("grp")
        copies = []
        for k, (t, s, layer, start, stop, offset) in enumerate(moves):
            columns, place = pl.ds(start, stop - start), pl.ds(offset, stop - start)
            if layer is None:
                source, target = ins[s].at[:, :, columns], outs[t].at[:, :, place]
            else:
                row = {"mine": me, "other": 1 - me}.get(layer, layer)
                source, target = ins[s].at[row, :, columns], outs[t].at[:, place]
            copies.append(pltpu.make_async_copy(source, target, sems.at[k]))
            copies[-1].start()
        for copy in copies:
            copy.wait()

    return pl.pallas_call(
        kernel,
        out_shape=shapes,
        in_specs=[ANYWHERE] * (count + len(after)),
        out_specs=[CHIP] * len(shapes),
        scratch_shapes=[pltpu.SemaphoreType.DMA((len(moves),))],
        compiler_params=pltpu.CompilerParams(vmem_limit_bytes=62 * MIB),
        cost_estimate=pl.CostEstimate(
            flops=0,
            transcendentals=0,
            bytes_accessed=4 * sum(math.prod(x.shape) * 2 for x in shapes),
        ),
    )(*sources, *after)


def cost(flops):
    return pl.CostEstimate(flops=flops, transcendentals=0, bytes_accessed=flops // 64)


class Loads:

    def __init__(self):
        self.arrays, self.keys = [], []

    def add(self, array, lead, first, width):
        for k, known in enumerate(self.arrays):
            if known is array:
                break
        else:
            k = len(self.arrays)
            self.arrays.append(array)
        self.keys.append((k, lead, first, width))
        return len(self.keys) - 1

    def scratch(self):
        buffers = [
            pltpu.VMEM((self.arrays[k].shape[-2], width), self.arrays[k].dtype)
            for k, _, _, width in self.keys
        ]
        return [*buffers, pltpu.SemaphoreType.DMA((len(self.keys),))]

    def start(self, ins, buffers):
        self.copies, self.refs = [], buffers[:-1]
        for i, (k, lead, first, width) in enumerate(self.keys):
            columns = pl.ds(first, width)
            row = lax.axis_index("grp") if lead == "mine" else lead
            source = ins[k].at[:, columns] if lead is None else ins[k].at[row, :, columns]
            self.copies.append(pltpu.make_async_copy(source, buffers[i], buffers[-1].at[i]))
            self.copies[-1].start()

    def wait(self, wanted):
        for i in sorted(set(wanted)):
            if self.copies[i] is not None:
                self.copies[i].wait()
                self.copies[i] = None


def products(total, tokens, factors, width):
    for a in range(0, width, SPAN):
        span = min(SPAN, width - a)
        left = rows_of([ref[:, first + a : first + a + span] for ref, first in tokens])
        right = rows_of([ref[:, first + a : first + a + span] for ref, first in factors])
        product = contract(left, right)
        total = product if total is None else total + product
    return total


def solution(mesh):
    blk = mesh.shape["blk"]
    chips = blk // 2
    full = (chips - 1) // 2
    order = chip_ring(chips)
    forward, backward = [], []
    for core in range(2):
        for k in range(chips):
            a = order[k] * 2 + core
            b = order[(k + 1) % chips] * 2 + core
            forward.append((a, b))
            backward.append((b, a))
    def swap_core(x):
        return lax.ppermute(x, "blk", [(i, i ^ 1) for i in range(blk)])

    def swap_grp(x):
        return lax.ppermute(x, "grp", [(0, 1), (1, 0)])

    def ahead_of(x):
        return lax.ppermute(x, "blk", forward)

    def back_of(x):
        return lax.ppermute(x, "blk", backward)

    def after(values, *others):
        return lax.optimization_barrier((*values, *others))[: len(values)]

    def shards(activations, backprops, out_factors, in_factors, lengths):
        tokens_here = activations.shape[1]
        width = backprops.shape[2]
        depth = activations.shape[2]
        cut = depth * 5 // 8
        packed = width + cut
        beyond = depth - cut
        columns = out_factors.shape[1]
        seq_count = lengths.shape[0]
        me = lax.axis_index("grp")
        device = lax.axis_index("blk")

        def packing(out_source, in_source, layer, start, stop):
            ranges = []
            if start < width:
                ranges.append((out_source, layer, start, min(stop, width)))
            if stop > width:
                ranges.append((in_source, layer, max(start - width, 0), stop - width))
            return ranges

        edges = [0, width // 2, width, packed]

        def away_part(k):
            return packing(1, 0, "other", edges[k], edges[k + 1])

        acts_sib, backs_sib = swap_core(activations), swap_core(backprops)

        sources = (activations, backprops)
        piece, *chunks = move(
            (*sources, out_factors, in_factors),
            [
                packing(2, 3, "mine", 0, packed) + [(3, k, cut, depth) for k in range(2)],
                away_part(0),
            ],
        )
        chunks += move(sources, [away_part(1), away_part(2)], after=(piece,))

        got = [piece]
        ahead = back = piece
        away, away_sib = [], []
        for step in range(full):
            given = [ahead, back]
            if step < 3:
                given.append(chunks[step])
            if step == 1:
                given = after(given, away[0], *chunks[1:], backs_sib)
            if step == 2:
                given = after(given, away[1], acts_sib)
                away_sib = [swap_core(x) for x in away]
            ahead, back = ahead_of(given[0]), back_of(given[1])
            if step < 3:
                away.append(swap_grp(given[2]))
            got += [ahead, back]
        total = packed + 2 * beyond
        middle = total // 2
        chip_tokens = 2 * tokens_here
        shard_rows = chips * columns
        if chips > 8:
            got = [jnp.concatenate(got, axis=0)]
        queries = columns * blk // RANK
        steps = [0]
        for k in range(1, full + 1):
            steps += [-k, k]
        steps.append(chips // 2)

        last = ahead_of(ahead[:, :middle]), back_of(back[:, middle:])
        away_sib.append(swap_core(after((away[2],), *last)[0]))
        own = ((backprops, backs_sib), (activations, acts_sib))
        lanes = -(-(shard_rows + 1) // 128) * 128

        def shard_pieces(loads, first, width):
            pieces = [loads.add(g, None, first, width) for g in got]
            if first < middle:
                return [*pieces, loads.add(last[0], None, first, width)]
            return [*pieces, loads.add(last[1], None, first - middle, width)]

        home_loads = Loads()
        home_plan = []
        for k in range(2):
            tokens = [home_loads.add(x, k, cut, beyond) for x in own[1]]
            home_plan.append((tokens, shard_pieces(home_loads, packed + k * beyond, beyond)))
        count_home = len(home_loads.arrays)

        def home_kernel(*refs):
            lengths_ref, mine_ref, other_ref, *scratch = refs[count_home:]
            home_loads.start(refs[:count_home], scratch)
            me = lax.axis_index("grp")
            first = lax.axis_index("blk") // 2 * chip_tokens
            limit = lengths_ref[first // LEN].astype(jnp.float32)
            for ref in (mine_ref, other_ref):
                ref[:, shard_rows:] = jnp.full((chip_tokens, lanes - shard_rows), limit)
            for k, sides in enumerate(home_plan):
                for side in sides:
                    home_loads.wait(side)
                tokens, factors = ([(home_loads.refs[i], 0) for i in side] for side in sides)
                value = products(None, tokens, factors, beyond)

                @pl.when(me == k)
                def _():
                    mine_ref[:, :shard_rows] = value

                @pl.when(me != k)
                def _():
                    other_ref[:, :shard_rows] = value

        extra = jax.ShapeDtypeStruct((chip_tokens, lanes), jnp.float32)
        home_mine, home_away = pl.pallas_call(
            home_kernel,
            out_shape=[extra] * 2,
            in_specs=[ANYWHERE] * count_home + [pl.BlockSpec(memory_space=pltpu.SMEM)],
            out_specs=[CHIP] * 2,
            scratch_shapes=home_loads.scratch(),
            compiler_params=pltpu.CompilerParams(vmem_limit_bytes=OUTER * MIB),
            cost_estimate=cost(2 * shard_rows * chip_tokens * 2 * beyond),
        )(*home_loads.arrays, lengths)
        home_away = swap_grp(home_away)

        main_loads = Loads()
        main_plan = []
        points = sorted({0, width // 2, width, middle, packed, *edges[1:]})
        for a, b in zip(points[:-1], points[1:]):
            k = max(i for i in range(3) if edges[i] <= a)
            side = int(a >= width)
            factors = shard_pieces(main_loads, a, b - a)
            tokens = [main_loads.add(x, "mine", a - side * width, b - a) for x in own[side]]
            tokens += [main_loads.add(x[k], None, a - edges[k], b - a) for x in (away, away_sib)]
            main_plan.append((side, tokens, factors, b - a))
        count_main = len(main_loads.arrays)

        def main_kernel(*refs):
            out_refs, scratch = refs[count_main : count_main + 2], refs[count_main + 2 :]
            main_loads.start(refs[:count_main], scratch)
            totals = [None, None]
            for side, tokens, factors, span in main_plan:
                main_loads.wait([*tokens, *factors])
                pieces = ([(main_loads.refs[i], 0) for i in x] for x in (tokens, factors))
                totals[side] = products(totals[side], *pieces, span)
            for ref, total in zip(out_refs, totals):
                ref[...] = total

        proj = jax.ShapeDtypeStruct((2 * chip_tokens, shard_rows), jnp.float32)
        proj_out, proj_in = pl.pallas_call(
            main_kernel,
            out_shape=[proj] * 2,
            in_specs=[ANYWHERE] * count_main,
            out_specs=[CHIP] * 2,
            scratch_shapes=main_loads.scratch(),
            compiler_params=pltpu.CompilerParams(vmem_limit_bytes=OUTER * MIB),
            cost_estimate=cost(2 * shard_rows * 2 * chip_tokens * packed),
        )(*main_loads.arrays)

        def score_kernel(*refs):
            out_ref, in_ref, mine_ref, other_ref, *scores = refs
            chip, odd = lax.axis_index("blk") // 2, lax.axis_index("blk") % 2
            at = jnp.where(chip % 2 == 0, chip // 2, chips - (chip + 1) // 2)
            within = lax.broadcasted_iota(jnp.int32, (columns, 128), 0)
            lowest = lax.broadcasted_iota(jnp.int32, (columns, 128), 1) * RANK
            hits = []
            for step in steps:
                p = (at + step + chips) % chips
                there = jnp.where(p < chips // 2, 2 * p, 2 * (chips - 1 - p) + 1)
                column = (there * 2 + odd) * columns + within
                hits.append(((column >= lowest) & (column < lowest + RANK)).astype(jnp.float32))
            hit = rows_of(hits)
            first = lax.axis_index("blk") // 2 * chip_tokens
            flip = lax.axis_index("blk") % 2
            row = lax.broadcasted_iota(jnp.int32, (chip_tokens, 1), 0)
            swapped = jnp.where(row < tokens_here, row + tokens_here, row - tokens_here)
            position = (first % LEN + jnp.where(flip == 1, swapped, row)).astype(jnp.float32)
            for k, extra_ref in enumerate((mine_ref, other_ref)):
                span = slice(k * chip_tokens, (k + 1) * chip_tokens)
                in_use = position < extra_ref[:, shard_rows : shard_rows + 1]
                product = out_ref[span, :] * (in_ref[span, :] + extra_ref[:, :shard_rows])
                product = jnp.where(in_use, product, 0.0)
                per_column = jnp.sum(product, axis=0, keepdims=True)
                scores[k][...] = lax.dot_general(
                    per_column,
                    hit,
                    (((1,), (0,)), ((), ())),
                    precision=lax.Precision.HIGHEST,
                    preferred_element_type=jnp.float32,
                )

        scored, other = pl.pallas_call(
            score_kernel,
            out_shape=[jax.ShapeDtypeStruct((1, 128), jnp.float32)] * 2,
            in_specs=[CHIP] * 4,
            out_specs=[CHIP] * 2,
            compiler_params=pltpu.CompilerParams(vmem_limit_bytes=RESERVE * MIB),
        )(proj_out, proj_in, home_mine, home_away)

        other = swap_grp(other)
        sequence = device // 2 * chip_tokens // LEN
        select = jnp.arange(seq_count, dtype=jnp.int32) == sequence
        rows = jnp.arange(2)[:, None] == me
        value = jnp.where(rows, scored, other)
        value = value[:, None, :] * select.astype(jnp.float32)[None, :, None]
        if blk & (blk - 1):
            return lax.psum(value, "blk")[:, :, :queries]
        bit = 1
        while bit < blk:
            value = value + lax.ppermute(value, "blk", [(i, i ^ bit) for i in range(blk)])
            bit *= 2
        return value[:, :, :queries]

    placed = (
        P(None, ("grp", "blk"), None),
        P(None, ("grp", "blk"), None),
        P(None, "blk", None),
        P(None, "blk", None),
        P("grp"),
    )
    return jax.shard_map(
        shards, mesh=mesh, in_specs=placed, out_specs=P(None, "grp", None), check_vma=False
    )
```

```python
import math

import jax
import jax.numpy as jnp
from jax import lax
from jax.experimental import pallas as pl
from jax.experimental.pallas import tpu as pltpu
from jax.sharding import PartitionSpec as P

RANK = 32
LEN = 2048
MIB = 2**20
SPAN = 512
RESERVE = 8
OUTER = 50
ANYWHERE = pl.BlockSpec(memory_space=pl.ANY)
CHIP = pl.BlockSpec(memory_space=pltpu.VMEM)


def chip_ring(chips):
    return list(range(0, chips, 2)) + list(range(chips - 1, 0, -2))


def contract(left, right):
    return lax.dot_general(
        left, right, (((1,), (1,)), ((), ())), preferred_element_type=jnp.float32
    )


def rows_of(pieces):
    return jnp.concatenate(pieces, axis=0) if len(pieces) > 1 else pieces[0]


def move(sources, targets, after=()):
    count = len(sources)
    moves, shapes = [], []
    for t, ranges in enumerate(targets):
        offset = 0
        for s, layer, start, stop in ranges:
            moves.append((t, s, layer, start, stop, offset))
            offset += stop - start
        lead = sources[s].shape[:2] if layer is None else sources[s].shape[1:2]
        shapes.append(jax.ShapeDtypeStruct((*lead, offset), sources[s].dtype))

    def kernel(*refs):
        ins, outs, sems = refs[:count], refs[count + len(after) : -1], refs[-1]
        me = lax.axis_index("grp")
        copies = []
        for k, (t, s, layer, start, stop, offset) in enumerate(moves):
            columns, place = pl.ds(start, stop - start), pl.ds(offset, stop - start)
            if layer is None:
                source, target = ins[s].at[:, :, columns], outs[t].at[:, :, place]
            else:
                row = {"mine": me, "other": 1 - me}.get(layer, layer)
                source, target = ins[s].at[row, :, columns], outs[t].at[:, place]
            copies.append(pltpu.make_async_copy(source, target, sems.at[k]))
            copies[-1].start()
        for copy in copies:
            copy.wait()

    return pl.pallas_call(
        kernel,
        out_shape=shapes,
        in_specs=[ANYWHERE] * (count + len(after)),
        out_specs=[CHIP] * len(shapes),
        scratch_shapes=[pltpu.SemaphoreType.DMA((len(moves),))],
        compiler_params=pltpu.CompilerParams(vmem_limit_bytes=62 * MIB),
        cost_estimate=pl.CostEstimate(
            flops=0,
            transcendentals=0,
            bytes_accessed=4 * sum(math.prod(x.shape) * 2 for x in shapes),
        ),
    )(*sources, *after)


def cost(flops):
    return pl.CostEstimate(flops=flops, transcendentals=0, bytes_accessed=flops // 64)


class Loads:

    def __init__(self):
        self.arrays, self.keys = [], []

    def add(self, array, lead, first, width):
        for k, known in enumerate(self.arrays):
            if known is array:
                break
        else:
            k = len(self.arrays)
            self.arrays.append(array)
        self.keys.append((k, lead, first, width))
        return len(self.keys) - 1

    def scratch(self):
        buffers = [
            pltpu.VMEM((self.arrays[k].shape[-2], width), self.arrays[k].dtype)
            for k, _, _, width in self.keys
        ]
        return [*buffers, pltpu.SemaphoreType.DMA((len(self.keys),))]

    def start(self, ins, buffers):
        self.copies, self.refs = [], buffers[:-1]
        for i, (k, lead, first, width) in enumerate(self.keys):
            columns = pl.ds(first, width)
            row = lax.axis_index("grp") if lead == "mine" else lead
            source = ins[k].at[:, columns] if lead is None else ins[k].at[row, :, columns]
            self.copies.append(pltpu.make_async_copy(source, buffers[i], buffers[-1].at[i]))
            self.copies[-1].start()

    def wait(self, wanted):
        for i in sorted(set(wanted)):
            if self.copies[i] is not None:
                self.copies[i].wait()
                self.copies[i] = None


def products(total, tokens, factors, width):
    for a in range(0, width, SPAN):
        span = min(SPAN, width - a)
        left = rows_of([ref[:, first + a : first + a + span] for ref, first in tokens])
        right = rows_of([ref[:, first + a : first + a + span] for ref, first in factors])
        product = contract(left, right)
        total = product if total is None else total + product
    return total


def solution(mesh):
    blk = mesh.shape["blk"]
    chips = blk // 2
    full = (chips - 1) // 2
    order = chip_ring(chips)
    forward, backward = [], []
    for core in range(2):
        for k in range(chips):
            a = order[k] * 2 + core
            b = order[(k + 1) % chips] * 2 + core
            forward.append((a, b))
            backward.append((b, a))
    def swap_core(x):
        return lax.ppermute(x, "blk", [(i, i ^ 1) for i in range(blk)])

    def swap_grp(x):
        return lax.ppermute(x, "grp", [(0, 1), (1, 0)])

    def ahead_of(x):
        return lax.ppermute(x, "blk", forward)

    def back_of(x):
        return lax.ppermute(x, "blk", backward)

    def after(values, *others):
        return lax.optimization_barrier((*values, *others))[: len(values)]

    def shards(activations, backprops, out_factors, in_factors, lengths):
        tokens_here = activations.shape[1]
        width = backprops.shape[2]
        depth = activations.shape[2]
        cut = depth * 5 // 8
        packed = width + cut
        beyond = depth - cut
        columns = out_factors.shape[1]
        seq_count = lengths.shape[0]
        me = lax.axis_index("grp")
        device = lax.axis_index("blk")

        def packing(out_source, in_source, layer, start, stop):
            ranges = []
            if start < width:
                ranges.append((out_source, layer, start, min(stop, width)))
            if stop > width:
                ranges.append((in_source, layer, max(start - width, 0), stop - width))
            return ranges

        edges = [0, width * 3 // 8, width * 7 // 8, packed]

        def away_part(k):
            return packing(1, 0, "other", edges[k], edges[k + 1])

        acts_sib, backs_sib = swap_core(activations), swap_core(backprops)

        sources = (activations, backprops)
        piece, *chunks = move(
            (*sources, out_factors, in_factors),
            [
                packing(2, 3, "mine", 0, packed) + [(3, k, cut, depth) for k in range(2)],
                away_part(0),
            ],
        )
        chunks += move(sources, [away_part(1), away_part(2)], after=(piece,))

        got = [piece]
        ahead = back = piece
        away, away_sib = [], []
        for step in range(full):
            ahead, back = ahead_of(ahead), back_of(back)
            if step < 3:
                chunk = chunks[step]
                if step:
                    chunk = after((chunk,), away[-1])[0]
                away.append(swap_grp(chunk))
            got += [ahead, back]
        away_sib = [swap_core(x) for x in away[:2]]
        total = packed + 2 * beyond
        middle = total // 2
        chip_tokens = 2 * tokens_here
        shard_rows = chips * columns
        if chips > 8:
            got = [jnp.concatenate(got, axis=0)]
        queries = columns * blk // RANK
        steps = [0]
        for k in range(1, full + 1):
            steps += [-k, k]
        steps.append(chips // 2)

        last = ahead_of(ahead[:, :middle]), back_of(back[:, middle:])
        away_sib.append(swap_core(after((away[2],), *last)[0]))
        own = ((backprops, backs_sib), (activations, acts_sib))
        lanes = -(-(shard_rows + 1) // 128) * 128

        def shard_pieces(loads, first, width):
            pieces = [loads.add(g, None, first, width) for g in got]
            if first < middle:
                return [*pieces, loads.add(last[0], None, first, width)]
            return [*pieces, loads.add(last[1], None, first - middle, width)]

        home_loads = Loads()
        home_plan = []
        for k in range(2):
            tokens = [home_loads.add(x, k, cut, beyond) for x in own[1]]
            home_plan.append((tokens, shard_pieces(home_loads, packed + k * beyond, beyond)))
        count_home = len(home_loads.arrays)

        def home_kernel(*refs):
            lengths_ref, mine_ref, other_ref, *scratch = refs[count_home:]
            home_loads.start(refs[:count_home], scratch)
            me = lax.axis_index("grp")
            first = lax.axis_index("blk") // 2 * chip_tokens
            limit = lengths_ref[first // LEN].astype(jnp.float32)
            for ref in (mine_ref, other_ref):
                ref[:, shard_rows:] = jnp.full((chip_tokens, lanes - shard_rows), limit)
            for k, sides in enumerate(home_plan):
                for side in sides:
                    home_loads.wait(side)
                tokens, factors = ([(home_loads.refs[i], 0) for i in side] for side in sides)
                value = products(None, tokens, factors, beyond)

                @pl.when(me == k)
                def _():
                    mine_ref[:, :shard_rows] = value

                @pl.when(me != k)
                def _():
                    other_ref[:, :shard_rows] = value

        extra = jax.ShapeDtypeStruct((chip_tokens, lanes), jnp.float32)
        home_mine, home_away = pl.pallas_call(
            home_kernel,
            out_shape=[extra] * 2,
            in_specs=[ANYWHERE] * count_home + [pl.BlockSpec(memory_space=pltpu.SMEM)],
            out_specs=[CHIP] * 2,
            scratch_shapes=home_loads.scratch(),
            compiler_params=pltpu.CompilerParams(vmem_limit_bytes=OUTER * MIB),
            cost_estimate=cost(2 * shard_rows * chip_tokens * 2 * beyond),
        )(*home_loads.arrays, lengths)
        home_away = swap_grp(home_away)

        main_loads = Loads()
        main_plan = []
        points = sorted({0, width // 2, width, middle, packed, *edges[1:]})
        for a, b in zip(points[:-1], points[1:]):
            k = max(i for i in range(3) if edges[i] <= a)
            side = int(a >= width)
            factors = shard_pieces(main_loads, a, b - a)
            tokens = [main_loads.add(x, "mine", a - side * width, b - a) for x in own[side]]
            tokens += [main_loads.add(x[k], None, a - edges[k], b - a) for x in (away, away_sib)]
            main_plan.append((side, tokens, factors, b - a))
        count_main = len(main_loads.arrays)

        def main_kernel(*refs):
            out_refs, scratch = refs[count_main : count_main + 2], refs[count_main + 2 :]
            main_loads.start(refs[:count_main], scratch)
            totals = [None, None]
            for side, tokens, factors, span in main_plan:
                main_loads.wait([*tokens, *factors])
                pieces = ([(main_loads.refs[i], 0) for i in x] for x in (tokens, factors))
                totals[side] = products(totals[side], *pieces, span)
            for ref, total in zip(out_refs, totals):
                ref[...] = total

        proj = jax.ShapeDtypeStruct((2 * chip_tokens, shard_rows), jnp.float32)
        proj_out, proj_in = pl.pallas_call(
            main_kernel,
            out_shape=[proj] * 2,
            in_specs=[ANYWHERE] * count_main,
            out_specs=[CHIP] * 2,
            scratch_shapes=main_loads.scratch(),
            compiler_params=pltpu.CompilerParams(vmem_limit_bytes=OUTER * MIB),
            cost_estimate=cost(2 * shard_rows * 2 * chip_tokens * packed),
        )(*main_loads.arrays)

        def score_kernel(*refs):
            out_ref, in_ref, mine_ref, other_ref, *scores = refs
            chip, odd = lax.axis_index("blk") // 2, lax.axis_index("blk") % 2
            at = jnp.where(chip % 2 == 0, chip // 2, chips - (chip + 1) // 2)
            within = lax.broadcasted_iota(jnp.int32, (columns, 128), 0)
            lowest = lax.broadcasted_iota(jnp.int32, (columns, 128), 1) * RANK
            hits = []
            for step in steps:
                p = (at + step + chips) % chips
                there = jnp.where(p < chips // 2, 2 * p, 2 * (chips - 1 - p) + 1)
                column = (there * 2 + odd) * columns + within
                hits.append(((column >= lowest) & (column < lowest + RANK)).astype(jnp.float32))
            hit = rows_of(hits)
            first = lax.axis_index("blk") // 2 * chip_tokens
            flip = lax.axis_index("blk") % 2
            row = lax.broadcasted_iota(jnp.int32, (chip_tokens, 1), 0)
            swapped = jnp.where(row < tokens_here, row + tokens_here, row - tokens_here)
            position = (first % LEN + jnp.where(flip == 1, swapped, row)).astype(jnp.float32)
            for k, extra_ref in enumerate((mine_ref, other_ref)):
                span = slice(k * chip_tokens, (k + 1) * chip_tokens)
                in_use = position < extra_ref[:, shard_rows : shard_rows + 1]
                product = out_ref[span, :] * (in_ref[span, :] + extra_ref[:, :shard_rows])
                product = jnp.where(in_use, product, 0.0)
                per_column = jnp.sum(product, axis=0, keepdims=True)
                scores[k][...] = lax.dot_general(
                    per_column,
                    hit,
                    (((1,), (0,)), ((), ())),
                    precision=lax.Precision.HIGHEST,
                    preferred_element_type=jnp.float32,
                )

        scored, other = pl.pallas_call(
            score_kernel,
            out_shape=[jax.ShapeDtypeStruct((1, 128), jnp.float32)] * 2,
            in_specs=[CHIP] * 4,
            out_specs=[CHIP] * 2,
            compiler_params=pltpu.CompilerParams(vmem_limit_bytes=RESERVE * MIB),
        )(proj_out, proj_in, home_mine, home_away)

        other = swap_grp(other)
        sequence = device // 2 * chip_tokens // LEN
        select = jnp.arange(seq_count, dtype=jnp.int32) == sequence
        rows = jnp.arange(2)[:, None] == me
        value = jnp.where(rows, scored, other)
        value = value[:, None, :] * select.astype(jnp.float32)[None, :, None]
        if blk & (blk - 1):
            return lax.psum(value, "blk")[:, :, :queries]
        bit = 1
        while bit < blk:
            value = value + lax.ppermute(value, "blk", [(i, i ^ bit) for i in range(blk)])
            bit *= 2
        return value[:, :, :queries]

    placed = (
        P(None, ("grp", "blk"), None),
        P(None, ("grp", "blk"), None),
        P(None, "blk", None),
        P(None, "blk", None),
        P("grp"),
    )
    return jax.shard_map(
        shards, mesh=mesh, in_specs=placed, out_specs=P(None, "grp", None), check_vma=False
    )
```

```python
import math

import jax
import jax.numpy as jnp
from jax import lax
from jax.experimental import pallas as pl
from jax.experimental.pallas import tpu as pltpu
from jax.sharding import PartitionSpec as P

RANK = 32
LEN = 2048
MIB = 2**20
SPAN = 512
RESERVE = 8
OUTER = 50
HOME = 60
LOAD = 4096
ANYWHERE = pl.BlockSpec(memory_space=pl.ANY)
CHIP = pl.BlockSpec(memory_space=pltpu.VMEM)


def chip_ring(chips):
    return list(range(0, chips, 2)) + list(range(chips - 1, 0, -2))


def contract(left, right):
    return lax.dot_general(
        left, right, (((1,), (1,)), ((), ())), preferred_element_type=jnp.float32
    )


def rows_of(pieces):
    return jnp.concatenate(pieces, axis=0) if len(pieces) > 1 else pieces[0]


def move(sources, targets, after=()):
    count = len(sources)
    moves, shapes = [], []
    for t, ranges in enumerate(targets):
        offset = 0
        for s, layer, start, stop in ranges:
            moves.append((t, s, layer, start, stop, offset))
            offset += stop - start
        lead = sources[s].shape[:2] if layer is None else sources[s].shape[1:2]
        shapes.append(jax.ShapeDtypeStruct((*lead, offset), sources[s].dtype))

    def kernel(*refs):
        ins, outs, sems = refs[:count], refs[count + len(after) : -1], refs[-1]
        me = lax.axis_index("grp")
        copies = []
        for k, (t, s, layer, start, stop, offset) in enumerate(moves):
            columns, place = pl.ds(start, stop - start), pl.ds(offset, stop - start)
            if layer is None:
                source, target = ins[s].at[:, :, columns], outs[t].at[:, :, place]
            else:
                row = {"mine": me, "other": 1 - me}.get(layer, layer)
                source, target = ins[s].at[row, :, columns], outs[t].at[:, place]
            copies.append(pltpu.make_async_copy(source, target, sems.at[k]))
            copies[-1].start()
        for copy in copies:
            copy.wait()

    return pl.pallas_call(
        kernel,
        out_shape=shapes,
        in_specs=[ANYWHERE] * (count + len(after)),
        out_specs=[CHIP] * len(shapes),
        scratch_shapes=[pltpu.SemaphoreType.DMA((len(moves),))],
        compiler_params=pltpu.CompilerParams(vmem_limit_bytes=60 * MIB),
        cost_estimate=pl.CostEstimate(
            flops=0,
            transcendentals=0,
            bytes_accessed=4 * sum(math.prod(x.shape) * 2 for x in shapes),
        ),
    )(*sources, *after)


def cost(flops):
    return pl.CostEstimate(flops=flops, transcendentals=0, bytes_accessed=flops // 64)


class Loads:

    def __init__(self):
        self.arrays, self.keys = [], []

    def add(self, array, lead, first, width):
        for k, known in enumerate(self.arrays):
            if known is array:
                break
        else:
            k = len(self.arrays)
            self.arrays.append(array)
        self.keys.append((k, lead, first, width))
        return len(self.keys) - 1

    def scratch(self):
        buffers = [
            pltpu.VMEM((self.arrays[k].shape[-2], width), self.arrays[k].dtype)
            for k, _, _, width in self.keys
        ]
        return [*buffers, pltpu.SemaphoreType.DMA((len(self.keys),))]

    def bind(self, ins, buffers):
        self.copies, self.refs = [], buffers[:-1]
        for i, (k, lead, first, width) in enumerate(self.keys):
            columns = pl.ds(first, width)
            row = lax.axis_index("grp") if lead == "mine" else lead
            source = ins[k].at[:, columns] if lead is None else ins[k].at[row, :, columns]
            self.copies.append(pltpu.make_async_copy(source, buffers[i], buffers[-1].at[i]))

    def start(self, wanted):
        for i in wanted:
            self.copies[i].start()

    def wait(self, wanted):
        for i in sorted(set(wanted)):
            if self.copies[i] is not None:
                self.copies[i].wait()
                self.copies[i] = None


def add_products(target, fresh, tokens, factors, width):
    for a in range(0, width, SPAN):
        span = min(SPAN, width - a)
        left = rows_of([ref[:, first + a : first + a + span] for ref, first in tokens])
        right = rows_of([ref[:, first + a : first + a + span] for ref, first in factors])
        product = contract(left, right)
        if fresh and a == 0:
            target[...] = product
        else:
            target[...] += product


def solution(mesh):
    blk = mesh.shape["blk"]
    chips = blk // 2
    full = (chips - 1) // 2
    order = chip_ring(chips)
    forward, backward = [], []
    for core in range(2):
        for k in range(chips):
            a = order[k] * 2 + core
            b = order[(k + 1) % chips] * 2 + core
            forward.append((a, b))
            backward.append((b, a))
    def swap_core(x):
        return lax.ppermute(x, "blk", [(i, i ^ 1) for i in range(blk)])

    def swap_grp(x):
        return lax.ppermute(x, "grp", [(0, 1), (1, 0)])

    def ahead_of(x):
        return lax.ppermute(x, "blk", forward)

    def back_of(x):
        return lax.ppermute(x, "blk", backward)

    def after(values, *others):
        return lax.optimization_barrier((*values, *others))[: len(values)]

    def shards(activations, backprops, out_factors, in_factors, lengths):
        tokens_here = activations.shape[1]
        width = backprops.shape[2]
        depth = activations.shape[2]
        cut = depth * 19 // 32
        packed = width + cut
        beyond = depth - cut
        columns = out_factors.shape[1]
        seq_count = lengths.shape[0]
        me = lax.axis_index("grp")
        device = lax.axis_index("blk")

        def packing(out_source, in_source, layer, start, stop):
            ranges = []
            if start < width:
                ranges.append((out_source, layer, start, min(stop, width)))
            if stop > width:
                ranges.append((in_source, layer, max(start - width, 0), stop - width))
            return ranges

        edges = [0, width * 6 // 16, width * 13 // 16, packed]

        def away_part(k):
            return packing(1, 0, "other", edges[k], edges[k + 1])

        acts_sib, backs_sib = swap_core(activations), swap_core(backprops)

        sources = (activations, backprops)
        piece, *chunks = move(
            (*sources, out_factors, in_factors),
            [
                packing(2, 3, "mine", 0, packed) + [(3, k, cut, depth) for k in range(2)],
                away_part(0),
            ],
        )
        chunks += move(sources, [away_part(1), away_part(2)], after=(piece,))

        got = [piece]
        ahead = back = piece
        away, away_sib = [], []
        for step in range(full):
            ahead, back = ahead_of(ahead), back_of(back)
            if step < 3:
                chunk = chunks[step]
                if step:
                    chunk = after((chunk,), away[-1])[0]
                away.append(swap_grp(chunk))
            got += [ahead, back]
        away_sib = [swap_core(x) for x in away[:2]]
        total = packed + 2 * beyond
        middle = total // 2
        chip_tokens = 2 * tokens_here
        shard_rows = chips * columns
        if chips > 8:
            got = [jnp.concatenate(got, axis=0)]
        queries = columns * blk // RANK
        steps = [0]
        for k in range(1, full + 1):
            steps += [-k, k]
        steps.append(chips // 2)

        last = ahead_of(ahead[:, :middle]), back_of(back[:, middle:])
        away_sib.append(swap_core(after((away[2],), *last)[0]))
        own = ((backprops, backs_sib), (activations, acts_sib))
        lanes = -(-(shard_rows + 1) // 128) * 128

        def shard_pieces(loads, first, width):
            pieces = [loads.add(g, None, first, width) for g in got]
            if first < middle:
                return [*pieces, loads.add(last[0], None, first, width)]
            return [*pieces, loads.add(last[1], None, first - middle, width)]

        home_loads = Loads()
        home_plan = []
        for k in range(2):
            tokens = [home_loads.add(x, k, cut, beyond) for x in own[1]]
            home_plan.append((tokens, shard_pieces(home_loads, packed + k * beyond, beyond)))
        count_home = len(home_loads.arrays)

        def home_kernel(*refs):
            lengths_ref, mine_ref, other_ref, total, *scratch = refs[count_home:]
            home_loads.bind(refs[:count_home], scratch)
            home_loads.start(range(len(home_loads.keys)))
            me = lax.axis_index("grp")
            first = lax.axis_index("blk") // 2 * chip_tokens
            limit = lengths_ref[first // LEN].astype(jnp.float32)
            for ref in (mine_ref, other_ref):
                ref[:, shard_rows:] = jnp.full((chip_tokens, lanes - shard_rows), limit)
            for k, sides in enumerate(home_plan):
                for side in sides:
                    home_loads.wait(side)
                tokens, factors = ([(home_loads.refs[i], 0) for i in side] for side in sides)
                add_products(total, True, tokens, factors, beyond)

                @pl.when(me == k)
                def _():
                    mine_ref[:, :shard_rows] = total[...]

                @pl.when(me != k)
                def _():
                    other_ref[:, :shard_rows] = total[...]

        extra = jax.ShapeDtypeStruct((chip_tokens, lanes), jnp.float32)
        home_mine, home_away = pl.pallas_call(
            home_kernel,
            out_shape=[extra] * 2,
            in_specs=[ANYWHERE] * count_home + [pl.BlockSpec(memory_space=pltpu.SMEM)],
            out_specs=[CHIP] * 2,
            scratch_shapes=[
                pltpu.VMEM((chip_tokens, shard_rows), jnp.float32),
                *home_loads.scratch(),
            ],
            compiler_params=pltpu.CompilerParams(vmem_limit_bytes=HOME * MIB),
            cost_estimate=cost(2 * shard_rows * chip_tokens * 2 * beyond),
        )(*home_loads.arrays, lengths)
        home_away = swap_grp(home_away)

        main_loads = Loads()
        main_plan = []
        points = sorted({*range(0, packed, LOAD), width, middle, packed, *edges[1:]})
        for a, b in zip(points[:-1], points[1:]):
            k = max(i for i in range(3) if edges[i] <= a)
            side = int(a >= width)
            factors = shard_pieces(main_loads, a, b - a)
            tokens = [main_loads.add(x, "mine", a - side * width, b - a) for x in own[side]]
            tokens += [main_loads.add(x[k], None, a - edges[k], b - a) for x in (away, away_sib)]
            main_plan.append((side, tokens, factors, b - a))
        count_main = len(main_loads.arrays)

        def main_kernel(*refs):
            out_refs, scratch = refs[count_main : count_main + 2], refs[count_main + 2 :]
            main_loads.bind(refs[:count_main], scratch)
            wanted = [[*tokens, *factors] for _, tokens, factors, _ in main_plan]
            for some in wanted:
                main_loads.start(some)
            for i, (side, tokens, factors, span) in enumerate(main_plan):
                main_loads.wait(wanted[i])
                pieces = ([(main_loads.refs[i], 0) for i in x] for x in (tokens, factors))
                add_products(out_refs[side], main_plan[i - 1][0] != side or not i, *pieces, span)

        proj = jax.ShapeDtypeStruct((2 * chip_tokens, shard_rows), jnp.float32)
        proj_out, proj_in = pl.pallas_call(
            main_kernel,
            out_shape=[proj] * 2,
            in_specs=[ANYWHERE] * count_main,
            out_specs=[CHIP] * 2,
            scratch_shapes=main_loads.scratch(),
            compiler_params=pltpu.CompilerParams(vmem_limit_bytes=OUTER * MIB),
            cost_estimate=cost(2 * shard_rows * 2 * chip_tokens * packed),
        )(*main_loads.arrays)

        def score_kernel(*refs):
            out_ref, in_ref, mine_ref, other_ref, *scores = refs
            chip, odd = lax.axis_index("blk") // 2, lax.axis_index("blk") % 2
            at = jnp.where(chip % 2 == 0, chip // 2, chips - (chip + 1) // 2)
            within = lax.broadcasted_iota(jnp.int32, (columns, 128), 0)
            lowest = lax.broadcasted_iota(jnp.int32, (columns, 128), 1) * RANK
            hits = []
            for step in steps:
                p = (at + step + chips) % chips
                there = jnp.where(p < chips // 2, 2 * p, 2 * (chips - 1 - p) + 1)
                column = (there * 2 + odd) * columns + within
                hits.append(((column >= lowest) & (column < lowest + RANK)).astype(jnp.float32))
            hit = rows_of(hits)
            first = lax.axis_index("blk") // 2 * chip_tokens
            flip = lax.axis_index("blk") % 2
            row = lax.broadcasted_iota(jnp.int32, (chip_tokens, 1), 0)
            swapped = jnp.where(row < tokens_here, row + tokens_here, row - tokens_here)
            position = (first % LEN + jnp.where(flip == 1, swapped, row)).astype(jnp.float32)
            for k, extra_ref in enumerate((mine_ref, other_ref)):
                span = slice(k * chip_tokens, (k + 1) * chip_tokens)
                in_use = position < extra_ref[:, shard_rows : shard_rows + 1]
                product = out_ref[span, :] * (in_ref[span, :] + extra_ref[:, :shard_rows])
                product = jnp.where(in_use, product, 0.0)
                per_column = jnp.sum(product, axis=0, keepdims=True)
                scores[k][...] = lax.dot_general(
                    per_column,
                    hit,
                    (((1,), (0,)), ((), ())),
                    precision=lax.Precision.HIGHEST,
                    preferred_element_type=jnp.float32,
                )

        scored, other = pl.pallas_call(
            score_kernel,
            out_shape=[jax.ShapeDtypeStruct((1, 128), jnp.float32)] * 2,
            in_specs=[CHIP] * 4,
            out_specs=[CHIP] * 2,
            compiler_params=pltpu.CompilerParams(vmem_limit_bytes=RESERVE * MIB),
        )(proj_out, proj_in, home_mine, home_away)

        other = swap_grp(other)
        sequence = device // 2 * chip_tokens // LEN
        select = jnp.arange(seq_count, dtype=jnp.int32) == sequence
        rows = jnp.arange(2)[:, None] == me
        value = jnp.where(rows, scored, other)
        value = value[:, None, :] * select.astype(jnp.float32)[None, :, None]
        if blk & (blk - 1):
            return lax.psum(value, "blk")[:, :, :queries]
        bit = 1
        while bit < blk:
            value = value + lax.ppermute(value, "blk", [(i, i ^ bit) for i in range(blk)])
            bit *= 2
        return value[:, :, :queries]

    placed = (
        P(None, ("grp", "blk"), None),
        P(None, ("grp", "blk"), None),
        P(None, "blk", None),
        P(None, "blk", None),
        P("grp"),
    )
    return jax.shard_map(
        shards, mesh=mesh, in_specs=placed, out_specs=P(None, "grp", None), check_vma=False
    )
```

```python
import math

import jax
import jax.numpy as jnp
from jax import lax
from jax.experimental import pallas as pl
from jax.experimental.pallas import tpu as pltpu
from jax.sharding import PartitionSpec as P

RANK = 32
LEN = 2048
MIB = 2**20
SPAN = 512
RESERVE = 8
OUTER = 52
HOME = 52
LOAD = 16384
ANYWHERE = pl.BlockSpec(memory_space=pl.ANY)
CHIP = pl.BlockSpec(memory_space=pltpu.VMEM)


def chip_ring(chips):
    return list(range(0, chips, 2)) + list(range(chips - 1, 0, -2))


def contract(left, right):
    return lax.dot_general(
        left, right, (((1,), (1,)), ((), ())), preferred_element_type=jnp.float32
    )


def rows_of(pieces):
    return jnp.concatenate(pieces, axis=0) if len(pieces) > 1 else pieces[0]


def move(sources, targets, after=()):
    count = len(sources)
    moves, shapes = [], []
    for t, ranges in enumerate(targets):
        offset = 0
        for s, layer, start, stop in ranges:
            moves.append((t, s, layer, start, stop, offset))
            offset += stop - start
        lead = sources[s].shape[:2] if layer is None else sources[s].shape[1:2]
        shapes.append(jax.ShapeDtypeStruct((*lead, offset), sources[s].dtype))

    def kernel(*refs):
        ins, outs, sems = refs[:count], refs[count + len(after) : -1], refs[-1]
        me = lax.axis_index("grp")
        copies = []
        for k, (t, s, layer, start, stop, offset) in enumerate(moves):
            columns, place = pl.ds(start, stop - start), pl.ds(offset, stop - start)
            if layer is None:
                source, target = ins[s].at[:, :, columns], outs[t].at[:, :, place]
            else:
                row = {"mine": me, "other": 1 - me}.get(layer, layer)
                source, target = ins[s].at[row, :, columns], outs[t].at[:, place]
            copies.append(pltpu.make_async_copy(source, target, sems.at[k]))
            copies[-1].start()
        for copy in copies:
            copy.wait()

    return pl.pallas_call(
        kernel,
        out_shape=shapes,
        in_specs=[ANYWHERE] * (count + len(after)),
        out_specs=[CHIP] * len(shapes),
        scratch_shapes=[pltpu.SemaphoreType.DMA((len(moves),))],
        compiler_params=pltpu.CompilerParams(vmem_limit_bytes=60 * MIB),
        cost_estimate=pl.CostEstimate(
            flops=0,
            transcendentals=0,
            bytes_accessed=4 * sum(math.prod(x.shape) * 2 for x in shapes),
        ),
    )(*sources, *after)


def cost(flops):
    return pl.CostEstimate(flops=flops, transcendentals=0, bytes_accessed=flops // 64)


class Loads:

    def __init__(self):
        self.arrays, self.keys = [], []

    def add(self, array, lead, first, width):
        for k, known in enumerate(self.arrays):
            if known is array:
                break
        else:
            k = len(self.arrays)
            self.arrays.append(array)
        self.keys.append((k, lead, first, width))
        return len(self.keys) - 1

    def scratch(self):
        buffers = [
            pltpu.VMEM((self.arrays[k].shape[-2], width), self.arrays[k].dtype)
            for k, _, _, width in self.keys
        ]
        return [*buffers, pltpu.SemaphoreType.DMA((len(self.keys),))]

    def bind(self, ins, buffers):
        self.copies, self.refs = [], buffers[:-1]
        for i, (k, lead, first, width) in enumerate(self.keys):
            columns = pl.ds(first, width)
            row = lax.axis_index("grp") if lead == "mine" else lead
            source = ins[k].at[:, columns] if lead is None else ins[k].at[row, :, columns]
            self.copies.append(pltpu.make_async_copy(source, buffers[i], buffers[-1].at[i]))

    def start(self, wanted):
        for i in wanted:
            self.copies[i].start()

    def wait(self, wanted):
        for i in sorted(set(wanted)):
            if self.copies[i] is not None:
                self.copies[i].wait()
                self.copies[i] = None


def add_products(target, fresh, tokens, factors, width):
    for a in range(0, width, SPAN):
        span = min(SPAN, width - a)
        left = rows_of([ref[:, first + a : first + a + span] for ref, first in tokens])
        right = rows_of([ref[:, first + a : first + a + span] for ref, first in factors])
        product = contract(left, right)
        if fresh and a == 0:
            target[...] = product
        else:
            target[...] += product


def solution(mesh):
    blk = mesh.shape["blk"]
    chips = blk // 2
    full = (chips - 1) // 2
    order = chip_ring(chips)
    forward, backward = [], []
    for core in range(2):
        for k in range(chips):
            a = order[k] * 2 + core
            b = order[(k + 1) % chips] * 2 + core
            forward.append((a, b))
            backward.append((b, a))
    def swap_core(x):
        return lax.ppermute(x, "blk", [(i, i ^ 1) for i in range(blk)])

    def swap_grp(x):
        return lax.ppermute(x, "grp", [(0, 1), (1, 0)])

    def ahead_of(x):
        return lax.ppermute(x, "blk", forward)

    def back_of(x):
        return lax.ppermute(x, "blk", backward)

    def after(values, *others):
        return lax.optimization_barrier((*values, *others))[: len(values)]

    def shards(activations, backprops, out_factors, in_factors, lengths):
        tokens_here = activations.shape[1]
        width = backprops.shape[2]
        depth = activations.shape[2]
        cut = depth * 19 // 32
        packed = width + cut
        beyond = depth - cut
        columns = out_factors.shape[1]
        seq_count = lengths.shape[0]
        me = lax.axis_index("grp")
        device = lax.axis_index("blk")

        def packing(out_source, in_source, layer, start, stop):
            ranges = []
            if start < width:
                ranges.append((out_source, layer, start, min(stop, width)))
            if stop > width:
                ranges.append((in_source, layer, max(start - width, 0), stop - width))
            return ranges

        edges = [0, width * 6 // 16, width * 13 // 16, packed]

        def away_part(k):
            return packing(1, 0, "other", edges[k], edges[k + 1])

        acts_sib, backs_sib = swap_core(activations), swap_core(backprops)

        sources = (activations, backprops)
        piece, *chunks = move(
            (*sources, out_factors, in_factors),
            [
                packing(2, 3, "mine", 0, packed) + [(3, k, cut, depth) for k in range(2)],
                away_part(0),
            ],
        )
        chunks += move(sources, [away_part(1), away_part(2)], after=(piece,))

        got = [piece]
        ahead = back = piece
        away, away_sib = [], []
        for step in range(full):
            ahead, back = ahead_of(ahead), back_of(back)
            if step < 3:
                chunk = chunks[step]
                if step:
                    chunk = after((chunk,), away[-1])[0]
                away.append(swap_grp(chunk))
            got += [ahead, back]
        away_sib = [swap_core(x) for x in away[:2]]
        total = packed + 2 * beyond
        middle = total // 2
        chip_tokens = 2 * tokens_here
        shard_rows = chips * columns
        if chips > 8:
            got = [jnp.concatenate(got, axis=0)]
        queries = columns * blk // RANK
        steps = [0]
        for k in range(1, full + 1):
            steps += [-k, k]
        steps.append(chips // 2)

        last = ahead_of(ahead[:, :middle]), back_of(back[:, middle:])
        away_sib.append(swap_core(after((away[2],), *last)[0]))
        own = ((backprops, backs_sib), (activations, acts_sib))
        lanes = -(-(shard_rows + 1) // 128) * 128

        def shard_pieces(loads, first, width):
            pieces = [loads.add(g, None, first, width) for g in got]
            if first < middle:
                return [*pieces, loads.add(last[0], None, first, width)]
            return [*pieces, loads.add(last[1], None, first - middle, width)]

        home_loads = Loads()
        home_plan = []
        for k in range(2):
            tokens = [home_loads.add(x, k, cut, beyond) for x in own[1]]
            home_plan.append((tokens, shard_pieces(home_loads, packed + k * beyond, beyond)))
        count_home = len(home_loads.arrays)

        def home_kernel(*refs):
            back_ref, lengths_ref, mine_ref, other_ref, held_ref, total, held_sem, *scratch = refs[
                count_home:
            ]
            held = pltpu.make_async_copy(
                back_ref.at[:, pl.ds(0, packed - middle)], held_ref, held_sem
            )
            home_loads.bind(refs[:count_home], scratch)
            home_loads.start(range(len(home_loads.keys)))
            held.start()
            me = lax.axis_index("grp")
            first = lax.axis_index("blk") // 2 * chip_tokens
            limit = lengths_ref[first // LEN].astype(jnp.float32)
            for ref in (mine_ref, other_ref):
                ref[:, shard_rows:] = jnp.full((chip_tokens, lanes - shard_rows), limit)
            for k, sides in enumerate(home_plan):
                for side in sides:
                    home_loads.wait(side)
                tokens, factors = ([(home_loads.refs[i], 0) for i in side] for side in sides)
                add_products(total, True, tokens, factors, beyond)

                @pl.when(me == k)
                def _():
                    mine_ref[:, :shard_rows] = total[...]

                @pl.when(me != k)
                def _():
                    other_ref[:, :shard_rows] = total[...]

            held.wait()

        extra = jax.ShapeDtypeStruct((chip_tokens, lanes), jnp.float32)
        home_mine, home_away, back_held = pl.pallas_call(
            home_kernel,
            out_shape=[
                extra,
                extra,
                jax.ShapeDtypeStruct((columns, packed - middle), last[1].dtype),
            ],
            in_specs=[ANYWHERE] * (count_home + 1) + [pl.BlockSpec(memory_space=pltpu.SMEM)],
            out_specs=[CHIP] * 3,
            scratch_shapes=[
                pltpu.VMEM((chip_tokens, shard_rows), jnp.float32),
                pltpu.SemaphoreType.DMA,
                *home_loads.scratch(),
            ],
            compiler_params=pltpu.CompilerParams(vmem_limit_bytes=HOME * MIB),
            cost_estimate=cost(2 * shard_rows * chip_tokens * 2 * beyond),
        )(*home_loads.arrays, last[1], lengths)
        home_away = swap_grp(home_away)

        last = (last[0], back_held)
        main_loads = Loads()
        main_plan = []
        points = sorted({*range(0, packed, LOAD), width, middle, packed, *edges[1:]})
        for a, b in zip(points[:-1], points[1:]):
            k = max(i for i in range(3) if edges[i] <= a)
            side = int(a >= width)
            factors = shard_pieces(main_loads, a, b - a)
            tokens = [main_loads.add(x, "mine", a - side * width, b - a) for x in own[side]]
            tokens += [main_loads.add(x[k], None, a - edges[k], b - a) for x in (away, away_sib)]
            main_plan.append((side, tokens, factors, b - a))
        count_main = len(main_loads.arrays)

        def main_kernel(*refs):
            out_refs, scratch = refs[count_main : count_main + 2], refs[count_main + 2 :]
            main_loads.bind(refs[:count_main], scratch)
            wanted = [[*tokens, *factors] for _, tokens, factors, _ in main_plan]
            for some in wanted:
                main_loads.start(some)
            for i, (side, tokens, factors, span) in enumerate(main_plan):
                main_loads.wait(wanted[i])
                pieces = ([(main_loads.refs[i], 0) for i in x] for x in (tokens, factors))
                add_products(out_refs[side], main_plan[i - 1][0] != side or not i, *pieces, span)

        proj = jax.ShapeDtypeStruct((2 * chip_tokens, shard_rows), jnp.float32)
        proj_out, proj_in = pl.pallas_call(
            main_kernel,
            out_shape=[proj] * 2,
            in_specs=[ANYWHERE] * count_main,
            out_specs=[CHIP] * 2,
            scratch_shapes=main_loads.scratch(),
            compiler_params=pltpu.CompilerParams(vmem_limit_bytes=OUTER * MIB),
            cost_estimate=cost(2 * shard_rows * 2 * chip_tokens * packed),
        )(*main_loads.arrays)

        def score_kernel(*refs):
            out_ref, in_ref, mine_ref, other_ref, *scores = refs
            chip, odd = lax.axis_index("blk") // 2, lax.axis_index("blk") % 2
            at = jnp.where(chip % 2 == 0, chip // 2, chips - (chip + 1) // 2)
            within = lax.broadcasted_iota(jnp.int32, (columns, 128), 0)
            lowest = lax.broadcasted_iota(jnp.int32, (columns, 128), 1) * RANK
            hits = []
            for step in steps:
                p = (at + step + chips) % chips
                there = jnp.where(p < chips // 2, 2 * p, 2 * (chips - 1 - p) + 1)
                column = (there * 2 + odd) * columns + within
                hits.append(((column >= lowest) & (column < lowest + RANK)).astype(jnp.float32))
            hit = rows_of(hits)
            first = lax.axis_index("blk") // 2 * chip_tokens
            flip = lax.axis_index("blk") % 2
            row = lax.broadcasted_iota(jnp.int32, (chip_tokens, 1), 0)
            swapped = jnp.where(row < tokens_here, row + tokens_here, row - tokens_here)
            position = (first % LEN + jnp.where(flip == 1, swapped, row)).astype(jnp.float32)
            for k, extra_ref in enumerate((mine_ref, other_ref)):
                span = slice(k * chip_tokens, (k + 1) * chip_tokens)
                in_use = position < extra_ref[:, shard_rows : shard_rows + 1]
                product = out_ref[span, :] * (in_ref[span, :] + extra_ref[:, :shard_rows])
                product = jnp.where(in_use, product, 0.0)
                per_column = jnp.sum(product, axis=0, keepdims=True)
                scores[k][...] = lax.dot_general(
                    per_column,
                    hit,
                    (((1,), (0,)), ((), ())),
                    precision=lax.Precision.HIGHEST,
                    preferred_element_type=jnp.float32,
                )

        scored, other = pl.pallas_call(
            score_kernel,
            out_shape=[jax.ShapeDtypeStruct((1, 128), jnp.float32)] * 2,
            in_specs=[CHIP] * 4,
            out_specs=[CHIP] * 2,
            compiler_params=pltpu.CompilerParams(vmem_limit_bytes=RESERVE * MIB),
        )(proj_out, proj_in, home_mine, home_away)

        other = swap_grp(other)
        sequence = device // 2 * chip_tokens // LEN
        select = jnp.arange(seq_count, dtype=jnp.int32) == sequence
        rows = jnp.arange(2)[:, None] == me
        value = jnp.where(rows, scored, other)
        value = value[:, None, :] * select.astype(jnp.float32)[None, :, None]
        if blk & (blk - 1):
            return lax.psum(value, "blk")[:, :, :queries]
        bit = 1
        while bit < blk:
            value = value + lax.ppermute(value, "blk", [(i, i ^ bit) for i in range(blk)])
            bit *= 2
        return value[:, :, :queries]

    placed = (
        P(None, ("grp", "blk"), None),
        P(None, ("grp", "blk"), None),
        P(None, "blk", None),
        P(None, "blk", None),
        P("grp"),
    )
    return jax.shard_map(
        shards, mesh=mesh, in_specs=placed, out_specs=P(None, "grp", None), check_vma=False
    )
```

```python
import math

import jax
import jax.numpy as jnp
from jax import lax
from jax.experimental import pallas as pl
from jax.experimental.pallas import tpu as pltpu
from jax.sharding import PartitionSpec as P

RANK = 32
LEN = 2048
MIB = 2**20
SPAN = 512
RESERVE = 8
OUTER = 52
HOME = 52
LOAD = 16384
ANYWHERE = pl.BlockSpec(memory_space=pl.ANY)
CHIP = pl.BlockSpec(memory_space=pltpu.VMEM)


def chip_ring(chips):
    return list(range(0, chips, 2)) + list(range(chips - 1, 0, -2))


def contract(left, right):
    return lax.dot_general(
        left, right, (((1,), (1,)), ((), ())), preferred_element_type=jnp.float32
    )


def rows_of(pieces):
    return jnp.concatenate(pieces, axis=0) if len(pieces) > 1 else pieces[0]


def move(sources, targets, after=()):
    count = len(sources)
    moves, shapes = [], []
    for t, ranges in enumerate(targets):
        offset = 0
        for s, layer, start, stop in ranges:
            moves.append((t, s, layer, start, stop, offset))
            offset += stop - start
        lead = sources[s].shape[:2] if layer is None else sources[s].shape[1:2]
        shapes.append(jax.ShapeDtypeStruct((*lead, offset), sources[s].dtype))

    def kernel(*refs):
        ins, outs, sems = refs[:count], refs[count + len(after) : -1], refs[-1]
        me = lax.axis_index("grp")
        copies = []
        for k, (t, s, layer, start, stop, offset) in enumerate(moves):
            columns, place = pl.ds(start, stop - start), pl.ds(offset, stop - start)
            if layer is None:
                source, target = ins[s].at[:, :, columns], outs[t].at[:, :, place]
            else:
                row = {"mine": me, "other": 1 - me}.get(layer, layer)
                source, target = ins[s].at[row, :, columns], outs[t].at[:, place]
            copies.append(pltpu.make_async_copy(source, target, sems.at[k]))
            copies[-1].start()
        for copy in copies:
            copy.wait()

    return pl.pallas_call(
        kernel,
        out_shape=shapes,
        in_specs=[ANYWHERE] * (count + len(after)),
        out_specs=[CHIP] * len(shapes),
        scratch_shapes=[pltpu.SemaphoreType.DMA((len(moves),))],
        compiler_params=pltpu.CompilerParams(vmem_limit_bytes=60 * MIB),
        cost_estimate=pl.CostEstimate(
            flops=0,
            transcendentals=0,
            bytes_accessed=4 * sum(math.prod(x.shape) * 2 for x in shapes),
        ),
    )(*sources, *after)


def cost(flops):
    return pl.CostEstimate(flops=flops, transcendentals=0, bytes_accessed=flops // 64)


class Loads:

    def __init__(self):
        self.arrays, self.keys = [], []

    def add(self, array, lead, first, width):
        for k, known in enumerate(self.arrays):
            if known is array:
                break
        else:
            k = len(self.arrays)
            self.arrays.append(array)
        self.keys.append((k, lead, first, width))
        return len(self.keys) - 1

    def scratch(self):
        buffers = [
            pltpu.VMEM((self.arrays[k].shape[-2], width), self.arrays[k].dtype)
            for k, _, _, width in self.keys
        ]
        return [*buffers, pltpu.SemaphoreType.DMA((len(self.keys),))]

    def bind(self, ins, buffers):
        self.copies, self.refs = [], buffers[:-1]
        for i, (k, lead, first, width) in enumerate(self.keys):
            columns = pl.ds(first, width)
            row = lax.axis_index("grp") if lead == "mine" else lead
            source = ins[k].at[:, columns] if lead is None else ins[k].at[row, :, columns]
            self.copies.append(pltpu.make_async_copy(source, buffers[i], buffers[-1].at[i]))

    def start(self, wanted):
        for i in wanted:
            self.copies[i].start()

    def wait(self, wanted):
        for i in sorted(set(wanted)):
            if self.copies[i] is not None:
                self.copies[i].wait()
                self.copies[i] = None


def add_products(target, fresh, tokens, factors, width):
    for a in range(0, width, SPAN):
        span = min(SPAN, width - a)
        left = rows_of([ref[:, first + a : first + a + span] for ref, first in tokens])
        right = rows_of([ref[:, first + a : first + a + span] for ref, first in factors])
        product = contract(left, right)
        if fresh and a == 0:
            target[...] = product
        else:
            target[...] += product


def solution(mesh):
    blk = mesh.shape["blk"]
    chips = blk // 2
    full = (chips - 1) // 2
    order = chip_ring(chips)
    forward, backward = [], []
    for core in range(2):
        for k in range(chips):
            a = order[k] * 2 + core
            b = order[(k + 1) % chips] * 2 + core
            forward.append((a, b))
            backward.append((b, a))
    def swap_core(x):
        return lax.ppermute(x, "blk", [(i, i ^ 1) for i in range(blk)])

    def swap_grp(x):
        return lax.ppermute(x, "grp", [(0, 1), (1, 0)])

    def ahead_of(x):
        return lax.ppermute(x, "blk", forward)

    def back_of(x):
        return lax.ppermute(x, "blk", backward)

    def after(values, *others):
        return lax.optimization_barrier((*values, *others))[: len(values)]

    def shards(activations, backprops, out_factors, in_factors, lengths):
        tokens_here = activations.shape[1]
        width = backprops.shape[2]
        depth = activations.shape[2]
        cut = depth * 19 // 32
        packed = width + cut
        beyond = depth - cut
        columns = out_factors.shape[1]
        seq_count = lengths.shape[0]
        me = lax.axis_index("grp")
        device = lax.axis_index("blk")

        def packing(out_source, in_source, layer, start, stop):
            ranges = []
            if start < width:
                ranges.append((out_source, layer, start, min(stop, width)))
            if stop > width:
                ranges.append((in_source, layer, max(start - width, 0), stop - width))
            return ranges

        edges = [0, width * 6 // 16, width * 12 // 16, packed]

        def away_part(k):
            return packing(1, 0, "other", edges[k], edges[k + 1])

        acts_sib, backs_sib = swap_core(activations), swap_core(backprops)

        sources = (activations, backprops)
        piece, *chunks = move(
            (*sources, out_factors, in_factors),
            [
                packing(2, 3, "mine", 0, packed) + [(3, k, cut, depth) for k in range(2)],
                away_part(0),
            ],
        )
        chunks += move(sources, [away_part(1), away_part(2)], after=(piece,))

        got = [piece]
        ahead = back = piece
        away, away_sib = [], []
        for step in range(full):
            ahead, back = ahead_of(ahead), back_of(back)
            if step < 3:
                chunk = chunks[step]
                if step:
                    chunk = after((chunk,), away[-1])[0]
                away.append(swap_grp(chunk))
            got += [ahead, back]
        away_sib = [swap_core(x) for x in away[:2]]
        total = packed + 2 * beyond
        middle = total // 2
        chip_tokens = 2 * tokens_here
        shard_rows = chips * columns
        if chips > 8:
            got = [jnp.concatenate(got, axis=0)]
        queries = columns * blk // RANK
        steps = [0]
        for k in range(1, full + 1):
            steps += [-k, k]
        steps.append(chips // 2)

        last = ahead_of(ahead[:, :middle]), back_of(back[:, middle:])
        away_sib.append(swap_core(after((away[2],), *last)[0]))
        own = ((backprops, backs_sib), (activations, acts_sib))
        lanes = -(-(shard_rows + 1) // 128) * 128

        def shard_pieces(loads, first, width):
            pieces = [loads.add(g, None, first, width) for g in got]
            if first < middle:
                return [*pieces, loads.add(last[0], None, first, width)]
            return [*pieces, loads.add(last[1], None, first - middle, width)]

        home_loads = Loads()
        home_plan = []
        for k in range(2):
            tokens = [home_loads.add(x, k, cut, beyond) for x in own[1]]
            home_plan.append((tokens, shard_pieces(home_loads, packed + k * beyond, beyond)))
        count_home = len(home_loads.arrays)

        def home_kernel(*refs):
            back_ref, lengths_ref, mine_ref, other_ref, held_ref, total, held_sem, *scratch = refs[
                count_home:
            ]
            held = pltpu.make_async_copy(
                back_ref.at[:, pl.ds(0, packed - middle)], held_ref, held_sem
            )
            home_loads.bind(refs[:count_home], scratch)
            home_loads.start(range(len(home_loads.keys)))
            held.start()
            me = lax.axis_index("grp")
            first = lax.axis_index("blk") // 2 * chip_tokens
            limit = lengths_ref[first // LEN].astype(jnp.float32)
            for ref in (mine_ref, other_ref):
                ref[:, shard_rows:] = jnp.full((chip_tokens, lanes - shard_rows), limit)
            for k, sides in enumerate(home_plan):
                for side in sides:
                    home_loads.wait(side)
                tokens, factors = ([(home_loads.refs[i], 0) for i in side] for side in sides)
                add_products(total, True, tokens, factors, beyond)

                @pl.when(me == k)
                def _():
                    mine_ref[:, :shard_rows] = total[...]

                @pl.when(me != k)
                def _():
                    other_ref[:, :shard_rows] = total[...]

            held.wait()

        extra = jax.ShapeDtypeStruct((chip_tokens, lanes), jnp.float32)
        home_mine, home_away, back_held = pl.pallas_call(
            home_kernel,
            out_shape=[
                extra,
                extra,
                jax.ShapeDtypeStruct((columns, packed - middle), last[1].dtype),
            ],
            in_specs=[ANYWHERE] * (count_home + 1) + [pl.BlockSpec(memory_space=pltpu.SMEM)],
            out_specs=[CHIP] * 3,
            scratch_shapes=[
                pltpu.VMEM((chip_tokens, shard_rows), jnp.float32),
                pltpu.SemaphoreType.DMA,
                *home_loads.scratch(),
            ],
            compiler_params=pltpu.CompilerParams(vmem_limit_bytes=HOME * MIB),
            cost_estimate=cost(2 * shard_rows * chip_tokens * 2 * beyond),
        )(*home_loads.arrays, last[1], lengths)
        home_away = swap_grp(home_away)

        last = (last[0], back_held)
        main_loads = Loads()
        main_plan = []
        points = sorted({*range(0, packed, LOAD), width, middle, packed, *edges[1:]})
        for a, b in zip(points[:-1], points[1:]):
            k = max(i for i in range(3) if edges[i] <= a)
            side = int(a >= width)
            factors = shard_pieces(main_loads, a, b - a)
            tokens = [main_loads.add(x, "mine", a - side * width, b - a) for x in own[side]]
            tokens += [main_loads.add(x[k], None, a - edges[k], b - a) for x in (away, away_sib)]
            main_plan.append((side, tokens, factors, b - a))
        count_main = len(main_loads.arrays)

        def main_kernel(*refs):
            out_refs, scratch = refs[count_main : count_main + 2], refs[count_main + 2 :]
            main_loads.bind(refs[:count_main], scratch)
            wanted = [[*tokens, *factors] for _, tokens, factors, _ in main_plan]
            for some in wanted:
                main_loads.start(some)
            for i, (side, tokens, factors, span) in enumerate(main_plan):
                main_loads.wait(wanted[i])
                pieces = ([(main_loads.refs[i], 0) for i in x] for x in (tokens, factors))
                add_products(out_refs[side], main_plan[i - 1][0] != side or not i, *pieces, span)

        proj = jax.ShapeDtypeStruct((2 * chip_tokens, shard_rows), jnp.float32)
        proj_out, proj_in = pl.pallas_call(
            main_kernel,
            out_shape=[proj] * 2,
            in_specs=[ANYWHERE] * count_main,
            out_specs=[CHIP] * 2,
            scratch_shapes=main_loads.scratch(),
            compiler_params=pltpu.CompilerParams(vmem_limit_bytes=OUTER * MIB),
            cost_estimate=cost(2 * shard_rows * 2 * chip_tokens * packed),
        )(*main_loads.arrays)

        def score_kernel(*refs):
            out_ref, in_ref, mine_ref, other_ref, *scores = refs
            chip, odd = lax.axis_index("blk") // 2, lax.axis_index("blk") % 2
            at = jnp.where(chip % 2 == 0, chip // 2, chips - (chip + 1) // 2)
            within = lax.broadcasted_iota(jnp.int32, (columns, 128), 0)
            lowest = lax.broadcasted_iota(jnp.int32, (columns, 128), 1) * RANK
            hits = []
            for step in steps:
                p = (at + step + chips) % chips
                there = jnp.where(p < chips // 2, 2 * p, 2 * (chips - 1 - p) + 1)
                column = (there * 2 + odd) * columns + within
                hits.append(((column >= lowest) & (column < lowest + RANK)).astype(jnp.float32))
            hit = rows_of(hits)
            first = lax.axis_index("blk") // 2 * chip_tokens
            flip = lax.axis_index("blk") % 2
            row = lax.broadcasted_iota(jnp.int32, (chip_tokens, 1), 0)
            swapped = jnp.where(row < tokens_here, row + tokens_here, row - tokens_here)
            position = (first % LEN + jnp.where(flip == 1, swapped, row)).astype(jnp.float32)
            for k, extra_ref in enumerate((mine_ref, other_ref)):
                span = slice(k * chip_tokens, (k + 1) * chip_tokens)
                in_use = position < extra_ref[:, shard_rows : shard_rows + 1]
                product = out_ref[span, :] * (in_ref[span, :] + extra_ref[:, :shard_rows])
                product = jnp.where(in_use, product, 0.0)
                per_column = jnp.sum(product, axis=0, keepdims=True)
                scores[k][...] = lax.dot_general(
                    per_column,
                    hit,
                    (((1,), (0,)), ((), ())),
                    precision=lax.Precision.HIGHEST,
                    preferred_element_type=jnp.float32,
                )

        scored, other = pl.pallas_call(
            score_kernel,
            out_shape=[jax.ShapeDtypeStruct((1, 128), jnp.float32)] * 2,
            in_specs=[CHIP] * 4,
            out_specs=[CHIP] * 2,
            compiler_params=pltpu.CompilerParams(vmem_limit_bytes=RESERVE * MIB),
        )(proj_out, proj_in, home_mine, home_away)

        other = swap_grp(other)
        sequence = device // 2 * chip_tokens // LEN
        select = jnp.arange(seq_count, dtype=jnp.int32) == sequence
        rows = jnp.arange(2)[:, None] == me
        value = jnp.where(rows, scored, other)
        value = value[:, None, :] * select.astype(jnp.float32)[None, :, None]
        if blk & (blk - 1):
            return lax.psum(value, "blk")[:, :, :queries]
        bit = 1
        while bit < blk:
            value = value + lax.ppermute(value, "blk", [(i, i ^ bit) for i in range(blk)])
            bit *= 2
        return value[:, :, :queries]

    placed = (
        P(None, ("grp", "blk"), None),
        P(None, ("grp", "blk"), None),
        P(None, "blk", None),
        P(None, "blk", None),
        P("grp"),
    )
    return jax.shard_map(
        shards, mesh=mesh, in_specs=placed, out_specs=P(None, "grp", None), check_vma=False
    )
```

```python
import math

import jax
import jax.numpy as jnp
from jax import lax
from jax.experimental import pallas as pl
from jax.experimental.pallas import tpu as pltpu
from jax.sharding import PartitionSpec as P

RANK = 32
LEN = 2048
MIB = 2**20
SPAN = 512
RESERVE = 8
OUTER = 52
HOME = 52
LOAD = 16384
ANYWHERE = pl.BlockSpec(memory_space=pl.ANY)
CHIP = pl.BlockSpec(memory_space=pltpu.VMEM)


def chip_ring(chips):
    return list(range(0, chips, 2)) + list(range(chips - 1, 0, -2))


def contract(left, right):
    return lax.dot_general(
        left, right, (((1,), (1,)), ((), ())), preferred_element_type=jnp.float32
    )


def rows_of(pieces):
    return jnp.concatenate(pieces, axis=0) if len(pieces) > 1 else pieces[0]


def move(sources, targets, after=()):
    count = len(sources)
    moves, shapes = [], []
    for t, ranges in enumerate(targets):
        offset = 0
        for s, layer, start, stop in ranges:
            moves.append((t, s, layer, start, stop, offset))
            offset += stop - start
        lead = sources[s].shape[:2] if layer is None else sources[s].shape[1:2]
        shapes.append(jax.ShapeDtypeStruct((*lead, offset), sources[s].dtype))

    def kernel(*refs):
        ins, outs, sems = refs[:count], refs[count + len(after) : -1], refs[-1]
        me = lax.axis_index("grp")
        copies = []
        for k, (t, s, layer, start, stop, offset) in enumerate(moves):
            columns, place = pl.ds(start, stop - start), pl.ds(offset, stop - start)
            if layer is None:
                source, target = ins[s].at[:, :, columns], outs[t].at[:, :, place]
            else:
                row = {"mine": me, "other": 1 - me}.get(layer, layer)
                source, target = ins[s].at[row, :, columns], outs[t].at[:, place]
            copies.append(pltpu.make_async_copy(source, target, sems.at[k]))
            copies[-1].start()
        for copy in copies:
            copy.wait()

    return pl.pallas_call(
        kernel,
        out_shape=shapes,
        in_specs=[ANYWHERE] * (count + len(after)),
        out_specs=[CHIP] * len(shapes),
        scratch_shapes=[pltpu.SemaphoreType.DMA((len(moves),))],
        compiler_params=pltpu.CompilerParams(vmem_limit_bytes=60 * MIB),
        cost_estimate=pl.CostEstimate(
            flops=0,
            transcendentals=0,
            bytes_accessed=4 * sum(math.prod(x.shape) * 2 for x in shapes),
        ),
    )(*sources, *after)


def cost(flops):
    return pl.CostEstimate(flops=flops, transcendentals=0, bytes_accessed=flops // 64)


class Loads:

    def __init__(self):
        self.arrays, self.keys = [], []

    def add(self, array, lead, first, width):
        for k, known in enumerate(self.arrays):
            if known is array:
                break
        else:
            k = len(self.arrays)
            self.arrays.append(array)
        self.keys.append((k, lead, first, width))
        return len(self.keys) - 1

    def scratch(self):
        buffers = [
            pltpu.VMEM((self.arrays[k].shape[-2], width), self.arrays[k].dtype)
            for k, _, _, width in self.keys
        ]
        return [*buffers, pltpu.SemaphoreType.DMA((len(self.keys),))]

    def bind(self, ins, buffers):
        self.copies, self.refs = [], buffers[:-1]
        for i, (k, lead, first, width) in enumerate(self.keys):
            columns = pl.ds(first, width)
            row = lax.axis_index("grp") if lead == "mine" else lead
            source = ins[k].at[:, columns] if lead is None else ins[k].at[row, :, columns]
            self.copies.append(pltpu.make_async_copy(source, buffers[i], buffers[-1].at[i]))

    def start(self, wanted):
        for i in wanted:
            self.copies[i].start()

    def wait(self, wanted):
        for i in sorted(set(wanted)):
            if self.copies[i] is not None:
                self.copies[i].wait()
                self.copies[i] = None


def add_products(target, fresh, tokens, factors, width):
    for a in range(0, width, SPAN):
        span = min(SPAN, width - a)
        left = rows_of([ref[:, first + a : first + a + span] for ref, first in tokens])
        right = rows_of([ref[:, first + a : first + a + span] for ref, first in factors])
        product = contract(left, right)
        if fresh and a == 0:
            target[...] = product
        else:
            target[...] += product


def solution(mesh):
    blk = mesh.shape["blk"]
    chips = blk // 2
    full = (chips - 1) // 2
    order = chip_ring(chips)
    forward, backward = [], []
    for core in range(2):
        for k in range(chips):
            a = order[k] * 2 + core
            b = order[(k + 1) % chips] * 2 + core
            forward.append((a, b))
            backward.append((b, a))
    def swap_core(x):
        return lax.ppermute(x, "blk", [(i, i ^ 1) for i in range(blk)])

    def swap_grp(x):
        return lax.ppermute(x, "grp", [(0, 1), (1, 0)])

    def ahead_of(x):
        return lax.ppermute(x, "blk", forward)

    def back_of(x):
        return lax.ppermute(x, "blk", backward)

    def after(values, *others):
        return lax.optimization_barrier((*values, *others))[: len(values)]

    def shards(activations, backprops, out_factors, in_factors, lengths):
        tokens_here = activations.shape[1]
        width = backprops.shape[2]
        depth = activations.shape[2]
        cut = depth * 37 // 64
        packed = width + cut
        beyond = depth - cut
        columns = out_factors.shape[1]
        seq_count = lengths.shape[0]
        me = lax.axis_index("grp")
        device = lax.axis_index("blk")

        def packing(out_source, in_source, layer, start, stop):
            ranges = []
            if start < width:
                ranges.append((out_source, layer, start, min(stop, width)))
            if stop > width:
                ranges.append((in_source, layer, max(start - width, 0), stop - width))
            return ranges

        edges = [0, width * 6 // 16, width * 12 // 16, packed]

        def away_part(k):
            return packing(1, 0, "other", edges[k], edges[k + 1])

        acts_sib, backs_sib = swap_core(activations), swap_core(backprops)

        sources = (activations, backprops)
        piece, *chunks = move(
            (*sources, out_factors, in_factors),
            [
                packing(2, 3, "mine", 0, packed) + [(3, k, cut, depth) for k in range(2)],
                away_part(0),
            ],
        )
        chunks += move(sources, [away_part(1), away_part(2)], after=(piece,))

        got = [piece]
        ahead = back = piece
        away, away_sib = [], []
        for step in range(full):
            ahead, back = ahead_of(ahead), back_of(back)
            if step < 3:
                chunk = chunks[step]
                if step:
                    chunk = after((chunk,), away[-1])[0]
                away.append(swap_grp(chunk))
            got += [ahead, back]
        away_sib = [swap_core(x) for x in away[:2]]
        total = packed + 2 * beyond
        middle = total // 256 * 128 - 128
        chip_tokens = 2 * tokens_here
        shard_rows = chips * columns
        if chips > 8:
            got = [jnp.concatenate(got, axis=0)]
        queries = columns * blk // RANK
        steps = [0]
        for k in range(1, full + 1):
            steps += [-k, k]
        steps.append(chips // 2)

        last = ahead_of(ahead[:, :middle]), back_of(back[:, middle:])
        away_sib.append(swap_core(after((away[2],), *last)[0]))
        own = ((backprops, backs_sib), (activations, acts_sib))
        lanes = -(-(shard_rows + 1) // 128) * 128

        def shard_pieces(loads, first, width):
            pieces = [loads.add(g, None, first, width) for g in got]
            if first < middle:
                return [*pieces, loads.add(last[0], None, first, width)]
            return [*pieces, loads.add(last[1], None, first - middle, width)]

        home_loads = Loads()
        home_plan = []
        for k in range(2):
            tokens = [home_loads.add(x, k, cut, beyond) for x in own[1]]
            home_plan.append((tokens, shard_pieces(home_loads, packed + k * beyond, beyond)))
        count_home = len(home_loads.arrays)

        def home_kernel(*refs):
            back_ref, lengths_ref, mine_ref, other_ref, held_ref, total, held_sem, *scratch = refs[
                count_home:
            ]
            held = pltpu.make_async_copy(
                back_ref.at[:, pl.ds(0, packed - middle)], held_ref, held_sem
            )
            home_loads.bind(refs[:count_home], scratch)
            home_loads.start(range(len(home_loads.keys)))
            held.start()
            me = lax.axis_index("grp")
            first = lax.axis_index("blk") // 2 * chip_tokens
            limit = lengths_ref[first // LEN].astype(jnp.float32)
            for ref in (mine_ref, other_ref):
                ref[:, shard_rows:] = jnp.full((chip_tokens, lanes - shard_rows), limit)
            for k, sides in enumerate(home_plan):
                for side in sides:
                    home_loads.wait(side)
                tokens, factors = ([(home_loads.refs[i], 0) for i in side] for side in sides)
                add_products(total, True, tokens, factors, beyond)

                @pl.when(me == k)
                def _():
                    mine_ref[:, :shard_rows] = total[...]

                @pl.when(me != k)
                def _():
                    other_ref[:, :shard_rows] = total[...]

            held.wait()

        extra = jax.ShapeDtypeStruct((chip_tokens, lanes), jnp.float32)
        home_mine, home_away, back_held = pl.pallas_call(
            home_kernel,
            out_shape=[
                extra,
                extra,
                jax.ShapeDtypeStruct((columns, packed - middle), last[1].dtype),
            ],
            in_specs=[ANYWHERE] * (count_home + 1) + [pl.BlockSpec(memory_space=pltpu.SMEM)],
            out_specs=[CHIP] * 3,
            scratch_shapes=[
                pltpu.VMEM((chip_tokens, shard_rows), jnp.float32),
                pltpu.SemaphoreType.DMA,
                *home_loads.scratch(),
            ],
            compiler_params=pltpu.CompilerParams(vmem_limit_bytes=HOME * MIB),
            cost_estimate=cost(2 * shard_rows * chip_tokens * 2 * beyond),
        )(*home_loads.arrays, last[1], lengths)
        home_away = swap_grp(home_away)

        last = (last[0], back_held)
        main_loads = Loads()
        main_plan = []
        points = sorted({*range(0, packed, LOAD), width, middle, packed, *edges[1:]})
        for a, b in zip(points[:-1], points[1:]):
            k = max(i for i in range(3) if edges[i] <= a)
            side = int(a >= width)
            factors = shard_pieces(main_loads, a, b - a)
            tokens = [main_loads.add(x, "mine", a - side * width, b - a) for x in own[side]]
            tokens += [main_loads.add(x[k], None, a - edges[k], b - a) for x in (away, away_sib)]
            main_plan.append((side, tokens, factors, b - a))
        count_main = len(main_loads.arrays)

        def main_kernel(*refs):
            out_refs, scratch = refs[count_main : count_main + 2], refs[count_main + 2 :]
            main_loads.bind(refs[:count_main], scratch)
            wanted = [[*tokens, *factors] for _, tokens, factors, _ in main_plan]
            for some in wanted:
                main_loads.start(some)
            for i, (side, tokens, factors, span) in enumerate(main_plan):
                main_loads.wait(wanted[i])
                pieces = ([(main_loads.refs[i], 0) for i in x] for x in (tokens, factors))
                add_products(out_refs[side], main_plan[i - 1][0] != side or not i, *pieces, span)

        proj = jax.ShapeDtypeStruct((2 * chip_tokens, shard_rows), jnp.float32)
        proj_out, proj_in = pl.pallas_call(
            main_kernel,
            out_shape=[proj] * 2,
            in_specs=[ANYWHERE] * count_main,
            out_specs=[CHIP] * 2,
            scratch_shapes=main_loads.scratch(),
            compiler_params=pltpu.CompilerParams(vmem_limit_bytes=OUTER * MIB),
            cost_estimate=cost(2 * shard_rows * 2 * chip_tokens * packed),
        )(*main_loads.arrays)

        def score_kernel(*refs):
            out_ref, in_ref, mine_ref, other_ref, *scores = refs
            chip, odd = lax.axis_index("blk") // 2, lax.axis_index("blk") % 2
            at = jnp.where(chip % 2 == 0, chip // 2, chips - (chip + 1) // 2)
            within = lax.broadcasted_iota(jnp.int32, (columns, 128), 0)
            lowest = lax.broadcasted_iota(jnp.int32, (columns, 128), 1) * RANK
            hits = []
            for step in steps:
                p = (at + step + chips) % chips
                there = jnp.where(p < chips // 2, 2 * p, 2 * (chips - 1 - p) + 1)
                column = (there * 2 + odd) * columns + within
                hits.append(((column >= lowest) & (column < lowest + RANK)).astype(jnp.float32))
            hit = rows_of(hits)
            first = lax.axis_index("blk") // 2 * chip_tokens
            flip = lax.axis_index("blk") % 2
            row = lax.broadcasted_iota(jnp.int32, (chip_tokens, 1), 0)
            swapped = jnp.where(row < tokens_here, row + tokens_here, row - tokens_here)
            position = (first % LEN + jnp.where(flip == 1, swapped, row)).astype(jnp.float32)
            for k, extra_ref in enumerate((mine_ref, other_ref)):
                span = slice(k * chip_tokens, (k + 1) * chip_tokens)
                in_use = position < extra_ref[:, shard_rows : shard_rows + 1]
                product = out_ref[span, :] * (in_ref[span, :] + extra_ref[:, :shard_rows])
                product = jnp.where(in_use, product, 0.0)
                per_column = jnp.sum(product, axis=0, keepdims=True)
                scores[k][...] = lax.dot_general(
                    per_column,
                    hit,
                    (((1,), (0,)), ((), ())),
                    precision=lax.Precision.HIGHEST,
                    preferred_element_type=jnp.float32,
                )

        scored, other = pl.pallas_call(
            score_kernel,
            out_shape=[jax.ShapeDtypeStruct((1, 128), jnp.float32)] * 2,
            in_specs=[CHIP] * 4,
            out_specs=[CHIP] * 2,
            compiler_params=pltpu.CompilerParams(vmem_limit_bytes=RESERVE * MIB),
        )(proj_out, proj_in, home_mine, home_away)

        other = swap_grp(other)
        sequence = device // 2 * chip_tokens // LEN
        select = jnp.arange(seq_count, dtype=jnp.int32) == sequence
        rows = jnp.arange(2)[:, None] == me
        value = jnp.where(rows, scored, other)
        value = value[:, None, :] * select.astype(jnp.float32)[None, :, None]
        if blk & (blk - 1):
            return lax.psum(value, "blk")[:, :, :queries]
        bit = 1
        while bit < blk:
            value = value + lax.ppermute(value, "blk", [(i, i ^ bit) for i in range(blk)])
            bit *= 2
        return value[:, :, :queries]

    placed = (
        P(None, ("grp", "blk"), None),
        P(None, ("grp", "blk"), None),
        P(None, "blk", None),
        P(None, "blk", None),
        P("grp"),
    )
    return jax.shard_map(
        shards, mesh=mesh, in_specs=placed, out_specs=P(None, "grp", None), check_vma=False
    )
```
